256 devices in a mesh: space: 128 (over z, y, x), col: 2 (over core).
Axes of the slice: x: 4, y: 4, z: 8, core: 2. Of those that a mesh axis runs over, the one named last changes fastest.
Arguments:
- block: float32 [96, 3, 512, 16, 128], P('col', None, 'space'), may hold values from -40 to 40, as said below
- material: int32 [512, 16, 128], P('space'), may hold values from 0 to 7
- eps_table: float32 [8], replicated, may hold values from 1 to 12
- edge_mask: int32 [3, 512, 16, 128], P(None, 'space'), may hold values 0 or 1
Outputs:
- residual: float32 [96, 3, 512, 16, 128], P('col', None, 'space')
- gram_a: float32 [96, 96], P('col')
- gram_b: float32 [96, 96], P('col')
- gram_flux: float32 [96, 96], P('col')
The draws below stay inside these ranges and needn't reach their ends.
Inputs may be any that keep to these rules, and one draw needn't show every extreme that they name: Entries of the block are bounded.
All inputs are finite; a program needn't handle non-finite values. No bound on the sum of `edge_mask` on one device may be relied on, other than what follows from the above.
Results may differ from the reference program's by a relative error of at most 0.000094.
Values sent between devices are 32-bit elements; how exact they have to be, the bound alone decides.
No kernel may reach another device: no remote copies, remote signals or barrier semaphores. Data moves between devices by JAX's collectives and lax.ppermute only.
A program may use at most 128 MiB of HBM per device.

```python
import math
import jax
import jax.numpy as jnp
from jax import lax

NC = 96
NMAT = 8
NX = 128
NY = 16
NZ = 512


def draw_block(key, part):
    key = jax.random.fold_in(key, 11)
    key_base, key_cell, key_column = jax.random.split(key, 3)
    shape = (NC, 3, NZ, NY, NX)
    cell_scale = jnp.exp(jax.random.uniform(key_cell, (1, 3, NZ, NY, NX), jnp.float32, -1.15, 1.15))
    column_scale = jnp.exp(jax.random.uniform(key_column, (NC, 1, 1, 1, 1), jnp.float32, -1.15, 1.15))
    base = jnp.clip(jax.random.normal(key_base, shape, jnp.float32), -4.0, 4.0)
    return jnp.clip(base * cell_scale * column_scale, -40.0, 40.0)


def touch_ends(entries, stream_key, least, high):
    longest = entries.shape.index(max(entries.shape))
    spots = []
    for shift in (0, 1):
        where = [jax.random.randint(jax.random.fold_in(stream_key, axis), (), 0, length) for axis, length in enumerate(entries.shape)]
        where[longest] = (where[longest] + shift) % entries.shape[longest]
        spots.append(tuple(where))
    return entries.at[spots[0]].set(least).at[spots[1]].set(high)


def setup_inputs(seed: int = 0) -> dict:
    seeds = jax.random.split(jax.random.key(seed), 5)
    block = draw_block(jax.random.fold_in(seeds[4], 71), 0)
    material = touch_ends(jax.random.randint(seeds[1], (NZ, NY, NX), 0, NMAT), jax.random.fold_in(seeds[1], 1), 0, NMAT - 1).astype(jnp.int32)
    eps_table = jnp.clip(jnp.exp(jax.random.uniform(seeds[2], (NMAT,), jnp.float32, math.log(1.0), math.log(12.0))), 1.0, 12.0)
    edge_mask = touch_ends((jax.random.randint(seeds[3], (3, NZ, NY, NX), 0, 16) < 15).astype(jnp.int32), jax.random.fold_in(seeds[3], 1), 0, 1)
    return {"block": block, "material": material, "eps_table": eps_table, "edge_mask": edge_mask}


def forward_diff(field, axis):
    size = field.shape[axis]
    ahead = lax.slice_in_dim(field, 1, size, axis=axis)
    widths = [(0, 0)] * field.ndim
    widths[axis] = (0, 1)
    return jnp.pad(ahead, widths) - field


def backward_diff(field, axis):
    size = field.shape[axis]
    behind = lax.slice_in_dim(field, 0, size - 1, axis=axis)
    widths = [(0, 0)] * field.ndim
    widths[axis] = (1, 0)
    return jnp.pad(behind, widths) - field


def curl_curl(padded):
    ex_low, ey_low, ez_low = padded[:, 0, :-1], padded[:, 1, :-1], padded[:, 2, :-1]
    ex_up, ey_up = padded[:, 0, 1:], padded[:, 1, 1:]
    hx_field = forward_diff(ez_low, 2) - (ey_up - ey_low)
    hy_field = (ex_up - ex_low) - forward_diff(ez_low, 3)
    hz_field = forward_diff(ey_low, 3) - forward_diff(ex_low, 2)
    kx_field = (hy_field[:, :-1] - hy_field[:, 1:]) - backward_diff(hz_field[:, 1:], 2)
    ky_field = backward_diff(hz_field[:, 1:], 3) - (hx_field[:, :-1] - hx_field[:, 1:])
    kz_field = backward_diff(hx_field[:, 1:], 2) - backward_diff(hy_field[:, 1:], 3)
    return jnp.stack([kx_field, ky_field, kz_field], axis=1)


def lookup(material, eps_table):
    eps = jnp.zeros(material.shape, jnp.float32)
    for index in range(eps_table.shape[0]):
        eps = eps + jnp.where(material == index, eps_table[index], jnp.float32(0.0))
    return eps


def reference(block, material, eps_table, edge_mask):
    keep = edge_mask.astype(jnp.float32)
    eps = lookup(material, eps_table)
    mass = eps[None] * keep
    inv_mass = keep / eps[None]
    masked = block * keep
    padded = jnp.pad(masked, ((0, 0), (0, 0), (1, 1), (0, 0), (0, 0)))
    image = curl_curl(padded) * keep
    mass_image = block * mass
    flux = image * inv_mass
    scale = 1.0 / (3.0 * NX * NY * NZ)
    hp = lax.Precision.HIGHEST
    flat_block = block.reshape(NC, -1)
    flat_image = image.reshape(NC, -1)
    gram_a = jnp.dot(flat_image, flat_block.T, precision=hp, preferred_element_type=jnp.float32) * scale
    gram_b = jnp.dot(mass_image.reshape(NC, -1), flat_block.T, precision=hp, preferred_element_type=jnp.float32) * scale
    gram_flux = jnp.dot(flux.reshape(NC, -1), flat_image.T, precision=hp, preferred_element_type=jnp.float32) * scale
    theta = jnp.diagonal(gram_a) / jnp.diagonal(gram_b)
    residual = image - theta[:, None, None, None, None] * mass_image
    return residual, gram_a, gram_b, gram_flux
```

```python
import functools

import jax
import jax.numpy as jnp
from jax import lax
from jax.experimental import pallas as pl
from jax.experimental.pallas import tpu as pltpu
from jax.sharding import PartitionSpec as P

MIB = 1 << 20
GRIDS = {128: (8, 4, 4), 8: (2, 2, 2)}
F32 = jnp.float32
BF16 = jnp.bfloat16
NT = (((1,), (1,)), ((), ()))


def forward(field, axis):
    size = field.shape[axis]
    ahead = pltpu.roll(field, size - 1, axis)
    at = lax.broadcasted_iota(jnp.int32, field.shape, axis)
    return jnp.where(at == size - 1, 0.0, ahead) - field


def backward(field, axis):
    size = field.shape[axis]
    behind = pltpu.roll(field, 1, axis)
    at = lax.broadcasted_iota(jnp.int32, field.shape, axis)
    return jnp.where(at == 0, 0.0, behind) - field


def lookup(material, table_ref):
    eps = jnp.zeros(material.shape, F32)
    for index in range(table_ref.shape[0]):
        eps = jnp.where(material == index, table_ref[index], eps)
    return eps


def split(value):
    high = value.astype(BF16)
    return high, (value - high.astype(F32)).astype(BF16)


def edges_kernel(first_ref, last_ref, keep_first_ref, keep_last_ref, one_ref, two_ref):
    core = lax.axis_index("col")
    kf = keep_first_ref[...].astype(F32)
    kl = keep_last_ref[...].astype(F32)
    down0 = first_ref[:, 0, 0] * kf[0, 0]
    down1 = first_ref[:, 1, 0] * kf[1, 0]
    ex = last_ref[:, 0, 0] * kl[0, 0]
    ey = last_ref[:, 1, 0] * kl[1, 0]
    ez = last_ref[:, 2, 0] * kl[2, 0]
    up0 = ex + forward(ez, 2)
    up1 = ey + forward(ez, 1)
    swap = core == 1
    one_ref[:, 0] = jnp.where(swap, down0, up0)
    one_ref[:, 1] = jnp.where(swap, down1, up1)
    two_ref[:, 0] = jnp.where(swap, up0, down0)
    two_ref[:, 1] = jnp.where(swap, up1, down1)


def edges(block, mask, chunk=8):
    ncol, _, nz, ny, nx = block.shape
    shape = jax.ShapeDtypeStruct((ncol, 2, ny, nx), F32)
    return pl.pallas_call(
        edges_kernel,
        grid=(ncol // chunk,),
        out_shape=(shape, shape),
        in_specs=[
            pl.BlockSpec((chunk, 3, 1, ny, nx), lambda i: (i, 0, 0, 0, 0)),
            pl.BlockSpec((chunk, 3, 1, ny, nx), lambda i: (i, 0, nz - 1, 0, 0)),
            pl.BlockSpec((3, 1, ny, nx), lambda i: (0, 0, 0, 0)),
            pl.BlockSpec((3, 1, ny, nx), lambda i: (0, nz - 1, 0, 0)),
        ],
        out_specs=[pl.BlockSpec((chunk, 2, ny, nx), lambda i: (i, 0, 0, 0))] * 2,
        compiler_params=pltpu.CompilerParams(vmem_limit_bytes=32 * MIB),
    )(block, block, mask, mask)


CHUNK = 16
LANES = 512


def store_rows(tmp_ref, dst_ref, row, ny, nx):
    per = LANES // nx
    for comp in range(3):
        for y in range(ny):
            rows = tmp_ref[comp, pl.ds(y, CHUNK, stride=ny), :]
            high, low = split(rows)
            at = (comp * ny + y) // per
            lanes = pl.ds(((comp * ny + y) % per) * nx, nx)
            dst_ref[at, pl.ds(row, CHUNK), lanes] = high
            dst_ref[at, pl.ds(128 + row, CHUNK), lanes] = low


def dots(left_ref, right_ref, acc_ref, steps, ncols, low):
    def step(k, carry):
        right = right_ref[k]
        acc = lax.dot_general(left_ref[k, 0:ncols, :], right, NT, preferred_element_type=F32)
        if low:
            acc += lax.dot_general(left_ref[k, 128 : 128 + ncols, :], right, NT, preferred_element_type=F32)
        acc_ref[...] += acc
        return carry

    lax.fori_loop(0, steps, step, 0)


def middle_kernel(
    own_ref, other_ref, mask_ref, material_ref, table_ref,
    near_own_ref, near_other_ref, edge_u_ref, acc_a_ref, acc_b_ref, acc_f_ref,
    keep_ref, root_ref, scale_ref, tmp_v, tmp_u, tmp_e, mid_u, mid_v,
):
    core = lax.axis_index("col")
    upper = core == 1
    step = pl.program_id(0)
    _, nz, ny, nx = mask_ref.shape
    ncols = 2 * CHUNK * pl.num_programs(0)
    half = near_own_ref.shape[0] * 3

    @pl.when(step == 0)
    def _():
        keep = mask_ref[...].astype(F32)
        root = jnp.sqrt(lookup(material_ref[...], table_ref))
        keep_ref[...] = keep
        root_ref[...] = root
        scale_ref[...] = keep / root[None]
        acc_a_ref[...] = jnp.zeros_like(acc_a_ref)
        acc_b_ref[...] = jnp.zeros_like(acc_b_ref)
        acc_f_ref[...] = jnp.zeros_like(acc_f_ref)

    def column(src_ref, near_ref, j):
        def e(comp, layer):
            return src_ref[j, comp, layer] * keep_ref[comp, layer]

        def dx(f):
            return forward(f, 1)

        def dy(f):
            return forward(f, 0)

        def bx(f):
            return backward(f, 1)

        def by(f):
            return backward(f, 0)

        x0, y0, z0 = (e(comp, core) for comp in range(3))
        x1, y1, z1 = (e(comp, core + 1) for comp in range(3))
        x2, y2 = (e(comp, core + 2) for comp in range(2))
        h01x = dy(z0) - (y1 - y0)
        h01y = (x1 - x0) - dx(z0)
        h12x = dy(z1) - (y2 - y1)
        h12y = (x2 - x1) - dx(z1)
        h1z = dx(y1) - dy(x1)
        rows = pl.ds(pl.multiple_of(j * ny, ny), ny)
        mid = core + 1
        tmp_v[0, rows, :] = ((h01y - h12y) - by(h1z)) * scale_ref[0, mid]
        tmp_v[1, rows, :] = (bx(h1z) - (h01x - h12x)) * scale_ref[1, mid]
        tmp_v[2, rows, :] = (by(h12x) - bx(h12y)) * scale_ref[2, mid]
        root = root_ref[mid]
        tmp_u[0, rows, :] = x1 * root
        tmp_u[1, rows, :] = y1 * root
        tmp_u[2, rows, :] = z1 * root
        edge = 3 * core
        xb, yb, zb = (e(comp, edge) for comp in range(3))
        hbz = dx(yb) - dy(xb)
        lowx = jnp.where(upper, h12x, -yb)
        lowy = jnp.where(upper, h12y, xb)
        topx = jnp.where(upper, dy(zb) + yb, h01x)
        topy = jnp.where(upper, -xb - dx(zb), h01y)
        near_ref[j, 0] = ((lowy - topy) - by(hbz)) * scale_ref[0, edge]
        near_ref[j, 1] = (bx(hbz) - (lowx - topx)) * scale_ref[1, edge]
        near_ref[j, 2] = (by(topx) - bx(topy)) * scale_ref[2, edge]
        root = root_ref[edge]
        tmp_e[0, rows, :] = xb * root
        tmp_e[1, rows, :] = yb * root
        tmp_e[2, rows, :] = zb * root

    total = edge_u_ref.shape[0]
    for src_ref, near_ref, side in ((own_ref, near_own_ref, core), (other_ref, near_other_ref, 1 - core)):
        def body(j, carry, src_ref=src_ref, near_ref=near_ref):
            column(src_ref, near_ref, j)
            return carry

        lax.fori_loop(0, CHUNK, body, 0)
        row = pl.multiple_of(side * half + step * CHUNK, CHUNK)
        store_rows(tmp_v, mid_v, row, ny, nx)
        store_rows(tmp_u, mid_u, row, ny, nx)
        store_rows(tmp_e, edge_u_ref, row, ny, nx)

    @pl.when(step == pl.num_programs(0) - 1)
    def _():
        n = 2 * half
        dots(mid_u, mid_v, acc_a_ref, total, n, True)
        dots(mid_v, mid_v, acc_f_ref, total, n, False)
        dots(mid_u, mid_u, acc_b_ref, total, n, False)
        dots(edge_u_ref, edge_u_ref, acc_b_ref, total, n, False)


def middle(block, other, mask, material, table):
    ncol, _, nz, ny, nx = block.shape
    total = 3 * ny * nx // LANES
    near = jax.ShapeDtypeStruct((ncol, 3, ny, nx), F32)
    acc = jax.ShapeDtypeStruct((2 * ncol, 256), F32)
    whole = lambda *shape: pl.BlockSpec(shape, lambda i: (0,) * len(shape))
    block_spec = pl.BlockSpec((CHUNK, 3, nz, ny, nx), lambda i: (i, 0, 0, 0, 0))
    near_spec = pl.BlockSpec((CHUNK, 3, ny, nx), lambda i: (i, 0, 0, 0))
    return pl.pallas_call(
        middle_kernel,
        grid=(ncol // CHUNK,),
        out_shape=(near, near, jax.ShapeDtypeStruct((total, 256, LANES), BF16), acc, acc, acc),
        in_specs=[
            block_spec, block_spec,
            whole(3, nz, ny, nx), whole(nz, ny, nx),
            pl.BlockSpec(memory_space=pltpu.SMEM),
        ],
        out_specs=[near_spec, near_spec, whole(total, 256, LANES)] + [whole(2 * ncol, 256)] * 3,
        scratch_shapes=[
            pltpu.VMEM((3, nz, ny, nx), F32),
            pltpu.VMEM((nz, ny, nx), F32),
            pltpu.VMEM((3, nz, ny, nx), F32),
            pltpu.VMEM((3, CHUNK * ny, nx), F32),
            pltpu.VMEM((3, CHUNK * ny, nx), F32),
            pltpu.VMEM((3, CHUNK * ny, nx), F32),
            pltpu.VMEM((total, 256, LANES), BF16),
            pltpu.VMEM((total, 256, LANES), BF16),
        ],
        compiler_params=pltpu.CompilerParams(vmem_limit_bytes=48 * MIB),
        cost_estimate=pl.CostEstimate(flops=2 * 10**9, bytes_accessed=16 * 10**6, transcendentals=0),
    )(block, other, mask, material, table)


def finish_kernel(
    near_own_ref, near_other_ref, halo_own_ref, halo_other_ref, mask_ref, material_ref, table_ref,
    edge_u_ref, acc_a_ref, acc_b_ref, acc_f_ref,
    keep_rows_ref, send_rows_ref,
    scale_ref, tmp_v, edge_v, sum_a, sum_f,
):
    core = lax.axis_index("col")
    step = pl.program_id(0)
    ny, nx = mask_ref.shape[2:]
    half = keep_rows_ref.shape[1]

    @pl.when(step == 0)
    def _():
        root = jnp.sqrt(lookup(material_ref[3 * core], table_ref))
        for comp in range(3):
            scale_ref[comp] = mask_ref[comp, 3 * core].astype(F32) / root
        sum_a[...] = acc_a_ref[...]
        sum_f[...] = acc_f_ref[...]

    weight = core.astype(F32)
    for near_ref, halo_ref, side in (
        (near_own_ref, halo_own_ref, core),
        (near_other_ref, halo_other_ref, 1 - core),
    ):
        def body(j, carry, near_ref=near_ref, halo_ref=halo_ref):
            h0 = halo_ref[j, 0]
            h1 = halo_ref[j, 1]
            rows = pl.ds(pl.multiple_of(j * ny, ny), ny)
            tmp_v[0, rows, :] = near_ref[j, 0] - h0 * scale_ref[0]
            tmp_v[1, rows, :] = near_ref[j, 1] - h1 * scale_ref[1]
            tmp_v[2, rows, :] = near_ref[j, 2] - (backward(h1, 0) + backward(h0, 1)) * (scale_ref[2] * weight)
            return carry

        lax.fori_loop(0, CHUNK, body, 0)
        store_rows(tmp_v, edge_v, pl.multiple_of(side * half + step * CHUNK, CHUNK), ny, nx)

    @pl.when(step == pl.num_programs(0) - 1)
    def _():
        n = 2 * half
        total = edge_v.shape[0]
        dots(edge_u_ref, edge_v, sum_a, total, n, True)
        dots(edge_v, edge_v, sum_f, total, n, False)
        sum_a[:, 0:n] = sum_a[:, 0:n] + sum_a[:, 128 : 128 + n]
        for ref, out in ((acc_b_ref, sum_a.at[:, 128:256]), (sum_f, sum_f.at[:, 0:128])):
            high = ref[:, 0:n]
            cross = ref[:, 128 : 128 + n]
            out[:, 0:n] = high + (cross + cross.T)
        own = pl.ds(pl.multiple_of(core * half, 8), half)
        its = pl.ds(pl.multiple_of((1 - core) * half, 8), half)
        for rows, out_ref in ((own, keep_rows_ref), (its, send_rows_ref)):
            out_ref[0] = sum_a[rows, 0:n]
            out_ref[1] = sum_a[rows, 128 : 128 + n]
            out_ref[2] = sum_f[rows, 0:n]


def finish(near_own, near_other, halo_own, halo_other, mask, material, table, edge_u, accs):
    ncol, _, ny, nx = near_own.shape
    nz = mask.shape[1]
    total = edge_u.shape[0]
    rows = jax.ShapeDtypeStruct((3, ncol, 2 * ncol), F32)
    whole = lambda *shape: pl.BlockSpec(shape, lambda i: (0,) * len(shape))
    near_spec = pl.BlockSpec((CHUNK, 3, ny, nx), lambda i: (i, 0, 0, 0))
    halo_spec = pl.BlockSpec((CHUNK, 2, ny, nx), lambda i: (i, 0, 0, 0))
    return pl.pallas_call(
        finish_kernel,
        grid=(ncol // CHUNK,),
        out_shape=(rows, rows),
        in_specs=[
            near_spec, near_spec, halo_spec, halo_spec,
            whole(3, nz, ny, nx), whole(nz, ny, nx),
            pl.BlockSpec(memory_space=pltpu.SMEM),
            whole(total, 256, LANES),
        ] + [whole(2 * ncol, 256)] * 3,
        out_specs=[whole(3, ncol, 2 * ncol)] * 2,
        scratch_shapes=[
            pltpu.VMEM((3, ny, nx), F32),
            pltpu.VMEM((3, CHUNK * ny, nx), F32),
            pltpu.VMEM((total, 256, LANES), BF16),
            pltpu.VMEM((2 * ncol, 256), F32),
            pltpu.VMEM((2 * ncol, 256), F32),
        ],
        compiler_params=pltpu.CompilerParams(vmem_limit_bytes=40 * MIB),
    )(near_own, near_other, halo_own, halo_other, mask, material, table, edge_u, *accs)


def image_kernel(block_ref, one_ref, two_ref, mask_ref, image_ref, keep_ref):
    core = lax.axis_index("col")
    upper = core == 1
    _, nz, ny, nx = mask_ref.shape

    @pl.when(pl.program_id(0) == 0)
    def _():
        keep_ref[...] = mask_ref[...].astype(F32)

    def body(j, carry):
        def e(comp, layer):
            return block_ref[j, comp, layer] * keep_ref[comp, layer]

        one0, one1, two0, two1 = one_ref[j, 0], one_ref[j, 1], two_ref[j, 0], two_ref[j, 1]
        x, y, z = (e(comp, 0) for comp in range(3))
        lowy = x - jnp.where(upper, two0, one0)
        lowx = jnp.where(upper, two1, one1) - y
        for layer in range(nz):
            if layer + 1 < nz:
                xn, yn, zn = (e(comp, layer + 1) for comp in range(3))
            else:
                xn, yn, zn = jnp.where(upper, one0, two0), jnp.where(upper, one1, two1), None
            topx = forward(z, 0) - (yn - y)
            topy = (xn - x) - forward(z, 1)
            hz = forward(y, 1) - forward(x, 0)
            image_ref[j, 0, layer] = ((lowy - topy) - backward(hz, 0)) * keep_ref[0, layer]
            image_ref[j, 1, layer] = (backward(hz, 1) - (lowx - topx)) * keep_ref[1, layer]
            image_ref[j, 2, layer] = (backward(topx, 0) - backward(topy, 1)) * keep_ref[2, layer]
            x, y, z, lowx, lowy = xn, yn, zn, topx, topy
        return carry

    lax.fori_loop(0, block_ref.shape[0], body, 0)


def image_of(block, one, two, mask, chunk=8):
    ncol, _, nz, ny, nx = block.shape
    block_spec = pl.BlockSpec((chunk, 3, nz, ny, nx), lambda i: (i, 0, 0, 0, 0))
    halo_spec = pl.BlockSpec((chunk, 2, ny, nx), lambda i: (i, 0, 0, 0))
    return pl.pallas_call(
        image_kernel,
        grid=(ncol // chunk,),
        out_shape=jax.ShapeDtypeStruct(block.shape, F32),
        in_specs=[
            block_spec, halo_spec, halo_spec,
            pl.BlockSpec((3, nz, ny, nx), lambda i: (0, 0, 0, 0)),
        ],
        out_specs=block_spec,
        scratch_shapes=[pltpu.VMEM((3, nz, ny, nx), F32)],
        compiler_params=pltpu.CompilerParams(vmem_limit_bytes=32 * MIB),
        cost_estimate=pl.CostEstimate(flops=10**9, bytes_accessed=11 * 10**6, transcendentals=0),
    )(block, one, two, mask)


def residual_kernel(
    scale, grams_ref, block_ref, image_ref, mask_ref, material_ref, table_ref,
    out_ref, ga_ref, gb_ref, gf_ref, mass_ref, theta_ref,
):
    core = lax.axis_index("col")
    step = pl.program_id(0)
    half, total = ga_ref.shape
    chunk = block_ref.shape[0]

    @pl.when(step == 0)
    def _():
        mass_ref[...] = lookup(material_ref[...], table_ref)[None] * mask_ref[...].astype(F32)
        ga = grams_ref[0] * scale
        gb = grams_ref[1] * scale
        ga_ref[...] = ga
        gb_ref[...] = gb
        gf_ref[...] = grams_ref[2] * scale
        rows = lax.broadcasted_iota(jnp.int32, (half, total), 0)
        cols = lax.broadcasted_iota(jnp.int32, (half, total), 1)
        here = cols == rows + core * half
        diag_a = jnp.sum(jnp.where(here, ga, 0.0), axis=1, keepdims=True)
        diag_b = jnp.sum(jnp.where(here, gb, 0.0), axis=1, keepdims=True)
        theta_ref[...] = jnp.broadcast_to(diag_a / diag_b, theta_ref.shape)

    def body(j, carry):
        theta = theta_ref[pl.ds(step * chunk + j, 1), :]
        out_ref[j] = image_ref[j] - theta[None, None] * (mass_ref[...] * block_ref[j])
        return carry

    lax.fori_loop(0, chunk, body, 0)


def residual_of(grams, block, image, mask, material, table, scale, chunk=8):
    ncol, _, nz, ny, nx = block.shape
    whole = lambda *shape: pl.BlockSpec(shape, lambda i: (0,) * len(shape))
    block_spec = pl.BlockSpec((chunk, 3, nz, ny, nx), lambda i: (i, 0, 0, 0, 0))
    gram = jax.ShapeDtypeStruct((ncol, 2 * ncol), F32)
    return pl.pallas_call(
        functools.partial(residual_kernel, scale),
        grid=(ncol // chunk,),
        out_shape=(jax.ShapeDtypeStruct(block.shape, F32), gram, gram, gram),
        in_specs=[
            whole(3, ncol, 2 * ncol), block_spec, block_spec,
            whole(3, nz, ny, nx), whole(nz, ny, nx),
            pl.BlockSpec(memory_space=pltpu.SMEM),
        ],
        out_specs=[block_spec] + [whole(ncol, 2 * ncol)] * 3,
        scratch_shapes=[pltpu.VMEM((3, nz, ny, nx), F32), pltpu.VMEM((ncol, nx), F32)],
        compiler_params=pltpu.CompilerParams(vmem_limit_bytes=32 * MIB),
        cost_estimate=pl.CostEstimate(flops=2 * 10**7, bytes_accessed=15 * 10**6, transcendentals=0),
    )(grams, block, image, mask, material, table)


def pair_rounds(slabs):
    nz, ny, nx = GRIDS[slabs]
    rounds = []
    for size, stride in ((nx, 1), (ny, nx), (nz, nx * ny)):
        for flip in {2: (1,), 4: (1, 3), 8: (1, 2, 7)}[size]:
            partner = lambda i: i + (((i // stride % size) ^ flip) - i // stride % size) * stride
            rounds.append([(i, partner(i)) for i in range(slabs)])
    return rounds


def shards(block, material, table, mask):
    slabs = lax.axis_size("space")
    ncol, _, nz, ny, nx = block.shape
    scale = 1.0 / (3.0 * nz * slabs * ny * nx)
    swap = [(0, 1), (1, 0)]
    other = lax.ppermute(block, "col", swap)
    one, two = edges(block, mask)
    ups = [(2 * i, 2 * i + 2) for i in range(slabs - 1)] + [(2 * i + 3, 2 * i + 1) for i in range(slabs - 1)]
    crossed = [(2 * i + 1, 2 * i + 2) for i in range(slabs - 1)] + [(2 * i + 2, 2 * i + 1) for i in range(slabs - 1)]
    halo_own = lax.ppermute(one, ("space", "col"), ups)
    halo_other = lax.ppermute(two, ("space", "col"), crossed)
    near_own, near_other, edge_u, *accs = middle(block, other, mask, material, table)
    keep_rows, send_rows = finish(near_own, near_other, halo_own, halo_other, mask, material, table, edge_u, accs)
    grams = keep_rows + lax.ppermute(send_rows, "col", swap)
    halo_far = lax.ppermute(halo_other, "col", swap)
    image = image_of(block, halo_own, halo_far, mask)
    for pairs in pair_rounds(slabs):
        grams = grams + lax.ppermute(grams, "space", pairs)
    return residual_of(grams, block, image, mask, material, table, scale)


def solution(mesh):
    in_specs = (
        P("col", None, "space", None, None),
        P("space", None, None),
        P(),
        P(None, "space", None, None),
    )
    out_specs = (
        P("col", None, "space", None, None),
        P("col", None),
        P("col", None),
        P("col", None),
    )
    return jax.shard_map(shards, mesh=mesh, in_specs=in_specs, out_specs=out_specs, check_vma=False)
```

```python
import functools

import jax
import jax.numpy as jnp
from jax import lax
from jax.experimental import pallas as pl
from jax.experimental.pallas import tpu as pltpu
from jax.sharding import PartitionSpec as P

MIB = 1 << 20
GRIDS = {128: (8, 4, 4), 8: (2, 2, 2)}
F32 = jnp.float32
BF16 = jnp.bfloat16
NT = (((1,), (1,)), ((), ()))
VMEM = pl.BlockSpec(memory_space=pltpu.VMEM)
SMEM = pl.BlockSpec(memory_space=pltpu.SMEM)
HBM = pl.BlockSpec(memory_space=pltpu.HBM)
GROUP = 16
LANES = 512


def lookup(material, table_ref):
    eps = jnp.zeros(material.shape, F32)
    for index in range(table_ref.shape[0]):
        eps = jnp.where(material == index, table_ref[index], eps)
    return eps


def split(value):
    high = value.astype(BF16)
    return high, (value - high.astype(F32)).astype(BF16)


def ahead_x(field):
    at = lax.broadcasted_iota(jnp.int32, field.shape, 1)
    size = field.shape[1]
    return jnp.where(at == size - 1, 0.0, pltpu.roll(field, size - 1, 1)) - field


def behind_x(field):
    at = lax.broadcasted_iota(jnp.int32, field.shape, 1)
    return jnp.where(at == 0, 0.0, pltpu.roll(field, 1, 1)) - field


def minus(left, right):
    return -right if left is None else left - right


def edges_kernel(block_ref, mask_ref, one_ref, two_ref, first_ref, last_ref, mask_first, mask_last, sems):
    ncol, _, nz, ny, nx = block_ref.shape
    copies = [
        pltpu.make_async_copy(mask_ref.at[0:2, 0], mask_first, sems.at[0]),
        pltpu.make_async_copy(mask_ref.at[:, nz - 1], mask_last, sems.at[1]),
        pltpu.make_async_copy(block_ref.at[:, 0:2, 0], first_ref, sems.at[2]),
        pltpu.make_async_copy(block_ref.at[:, :, nz - 1], last_ref, sems.at[3]),
    ]
    for copy in copies:
        copy.start()
    for copy in copies:
        copy.wait()
    swap = lax.axis_index("col") == 1
    first = first_ref.reshape(ncol * 2 * ny, nx)
    last = last_ref.reshape(ncol * 3 * ny, nx)

    def low(comp, y):
        keep = mask_first[comp, y : y + 1, :].astype(F32)
        return first[pl.ds(comp * ny + y, ncol, stride=2 * ny), :] * keep

    def high(comp, y):
        keep = mask_last[comp, y : y + 1, :].astype(F32)
        return last[pl.ds(comp * ny + y, ncol, stride=3 * ny), :] * keep

    ez = high(2, 0)
    for y in range(ny):
        ez_next = high(2, y + 1) if y + 1 < ny else None
        up0 = high(0, y) + ahead_x(ez)
        up1 = high(1, y) + minus(ez_next, ez)
        down0 = low(0, y)
        down1 = low(1, y)
        one_ref[0, y] = jnp.where(swap, down0, up0)
        one_ref[1, y] = jnp.where(swap, down1, up1)
        two_ref[0, y] = jnp.where(swap, up0, down0)
        two_ref[1, y] = jnp.where(swap, up1, down1)
        ez = ez_next


def edges(block, mask):
    ncol, _, nz, ny, nx = block.shape
    shape = jax.ShapeDtypeStruct((2, ny, ncol, nx), F32)
    return pl.pallas_call(
        edges_kernel,
        out_shape=(shape, shape),
        in_specs=[HBM, HBM],
        out_specs=[VMEM, VMEM],
        scratch_shapes=[
            pltpu.VMEM((ncol, 2, ny, nx), F32),
            pltpu.VMEM((ncol, 3, ny, nx), F32),
            pltpu.VMEM((2, ny, nx), jnp.int32),
            pltpu.VMEM((3, ny, nx), jnp.int32),
            pltpu.SemaphoreType.DMA((4,)),
        ],
        compiler_params=pltpu.CompilerParams(vmem_limit_bytes=61 * MIB),
    )(block, mask)


def place(comp, y, ny, nx):
    at = (comp * ny + y) * nx
    return at // LANES, pl.ds(at % LANES, nx)


def put_v(ref, row, comp, y, ny, value):
    at, lanes = place(comp, y, ny, value.shape[1])
    high, low = split(value)
    ref[at, pl.ds(row, GROUP), lanes] = low
    ref[at, pl.ds(128 + row, GROUP), lanes] = high


def put_u(ref, row, comp, y, ny, half, value):
    at, lanes = place(comp, y, ny, value.shape[1])
    high, low = split(value)
    ref[at, pl.ds(row, GROUP), lanes] = high
    ref[at, pl.ds(2 * half + row, GROUP), lanes] = low


def dots_uv(u_ref, v_ref, acc_ref, half):
    def step(k, carry):
        left = jnp.concatenate([v_ref[k, 128 : 128 + 2 * half, :], u_ref[k]], axis=0)
        acc_ref[...] += lax.dot_general(left, v_ref[k], NT, preferred_element_type=F32)
        return carry

    lax.fori_loop(0, u_ref.shape[0], step, 0, unroll=4)


def dots_uu(u_ref, acc_ref, half):
    def step(k, carry):
        acc_ref[...] += lax.dot_general(u_ref[k, 0 : 2 * half, :], u_ref[k], NT, preferred_element_type=F32)
        return carry

    lax.fori_loop(0, u_ref.shape[0], step, 0, unroll=4)


def middle_kernel(
    own_ref, other_ref, mask_ref, material_ref, table_ref,
    near_ref, edge_u_ref, acc_v_ref, acc_u_ref,
    keep_ref, root_ref, scale_ref, mid_u, mid_v,
):
    core = lax.axis_index("col")
    upper = core == 1
    step = pl.program_id(0)
    _, nz, ny, nx = mask_ref.shape
    half = near_ref.shape[2] // 2
    edge = 3 * core

    @pl.when(step == 0)
    def _():
        keep = mask_ref[...].astype(F32)
        root = jnp.sqrt(lookup(material_ref[...], table_ref))
        keep_ref[...] = keep
        root_ref[...] = root
        scale_ref[...] = keep / root[None]
        acc_v_ref[...] = jnp.zeros_like(acc_v_ref)
        acc_u_ref[...] = jnp.zeros_like(acc_u_ref)
        mid_v[...] = jnp.zeros_like(mid_v)

    for src, side in ((own_ref, core), (other_ref, 1 - core)):
        cells = src.reshape(GROUP * 3 * nz * ny, nx)
        row = pl.multiple_of(side * half + step * GROUP, GROUP)

        def e(comp, layer, y):
            value = cells[pl.ds((comp * nz + layer) * ny + y, GROUP, stride=3 * nz * ny), :]
            return value * keep_ref[comp, layer, y : y + 1, :]

        def row_of(y):
            window = [[e(comp, core + w, y) for comp in range(3)] for w in range(2)]
            window.append([e(comp, core + 2, y) for comp in range(2)])
            return window, [e(comp, edge, y) for comp in range(3)]

        here = row_of(0)
        last = (None,) * 5
        for y in range(ny):
            if y + 1 < ny:
                after = row_of(y + 1)
                (_, _, z0n), (x1n, _, z1n), _ = after[0]
                xbn, _, zbn = after[1]
            else:
                after, z0n, x1n, z1n, xbn, zbn = (None,) * 6
            ((x0, y0, z0), (x1, y1, z1), (x2, y2)), (xb, yb, zb) = here
            h01x = minus(z0n, z0) - (y1 - y0)
            h01y = (x1 - x0) - ahead_x(z0)
            h12x = minus(z1n, z1) - (y2 - y1)
            h12y = (x2 - x1) - ahead_x(z1)
            h1z = ahead_x(y1) - minus(x1n, x1)
            hbz = ahead_x(yb) - minus(xbn, xb)
            lowx = jnp.where(upper, h12x, -yb)
            lowy = jnp.where(upper, h12y, xb)
            topx = jnp.where(upper, minus(zbn, zb) + yb, h01x)
            topy = jnp.where(upper, -xb - ahead_x(zb), h01y)
            h1z_last, h12x_last, hbz_last, topx_last, _ = last
            mid = core + 1
            k = (
                (h01y - h12y) - minus(h1z_last, h1z),
                behind_x(h1z) - (h01x - h12x),
                minus(h12x_last, h12x) - behind_x(h12y),
            )
            kb = (
                (lowy - topy) - minus(hbz_last, hbz),
                behind_x(hbz) - (lowx - topx),
                minus(topx_last, topx) - behind_x(topy),
            )
            root_mid = root_ref[mid, y : y + 1, :]
            root_edge = root_ref[edge, y : y + 1, :]
            for comp in range(3):
                put_v(mid_v, row, comp, y, ny, k[comp] * scale_ref[comp, mid, y : y + 1, :])
                put_u(mid_u, row, comp, y, ny, half, (x1, y1, z1)[comp] * root_mid)
                near_ref[comp, y, pl.ds(row, GROUP), :] = kb[comp] * scale_ref[comp, edge, y : y + 1, :]
                put_u(edge_u_ref, row, comp, y, ny, half, (xb, yb, zb)[comp] * root_edge)
            last = (h1z, h12x, hbz, topx, None)
            here = after

    @pl.when(step == pl.num_programs(0) - 1)
    def _():
        dots_uv(mid_u, mid_v, acc_v_ref, half)
        dots_uu(mid_u, acc_u_ref, half)
        dots_uu(edge_u_ref, acc_u_ref, half)


def middle(block, other, mask, material, table):
    ncol, _, nz, ny, nx = block.shape
    total = 3 * ny * nx // LANES
    near = jax.ShapeDtypeStruct((3, ny, 2 * ncol, nx), F32)
    whole = lambda *shape: pl.BlockSpec(shape, lambda i: (0,) * len(shape))
    block_spec = pl.BlockSpec((GROUP, 3, nz, ny, nx), lambda i: (i, 0, 0, 0, 0))
    outs = [
        jax.ShapeDtypeStruct((3, ny, 2 * ncol, nx), F32),
        jax.ShapeDtypeStruct((total, 4 * ncol, LANES), BF16),
        jax.ShapeDtypeStruct((6 * ncol, 256), F32),
        jax.ShapeDtypeStruct((2 * ncol, 4 * ncol), F32),
    ]
    return pl.pallas_call(
        middle_kernel,
        grid=(ncol // GROUP,),
        out_shape=outs,
        in_specs=[block_spec, block_spec, whole(3, nz, ny, nx), whole(nz, ny, nx), SMEM],
        out_specs=[whole(*out.shape) for out in outs],
        scratch_shapes=[
            pltpu.VMEM((3, nz, ny, nx), F32),
            pltpu.VMEM((nz, ny, nx), F32),
            pltpu.VMEM((3, nz, ny, nx), F32),
            pltpu.VMEM((total, 4 * ncol, LANES), BF16),
            pltpu.VMEM((total, 256, LANES), BF16),
        ],
        compiler_params=pltpu.CompilerParams(vmem_limit_bytes=36 * MIB),
        cost_estimate=pl.CostEstimate(flops=2 * 10**9, bytes_accessed=16 * 10**6, transcendentals=0),
    )(block, other, mask, material, table)


def pack(core, swap, ga, gb, gf, rows, half):
    out = []
    for gram in (ga, gb, gf):
        part = gram[rows, :]
        left, right = part[:, 0:half], part[:, half : 2 * half]
        out.append((jnp.where(swap, right, left), jnp.where(swap, left, right)))
    down = lax.broadcasted_iota(jnp.int32, (half, half), 0)
    across = lax.broadcasted_iota(jnp.int32, (half, half), 1)
    (aa, ab), (ba, bb), (fa, fb) = out
    diag = jnp.sum(jnp.where(down == across, ba, 0.0), axis=1, keepdims=True)
    mixed = jnp.where(across <= down, aa, ba)
    return jnp.concatenate([mixed, fa, ab, bb, fb, jnp.broadcast_to(diag, (half, 256 - 5 * half))], axis=1)


def finish_kernel(
    near_ref, halo_own_ref, halo_other_ref, mask_ref, material_ref, table_ref,
    edge_u_ref, acc_v_ref, acc_u_ref,
    keep_rows_ref, send_rows_ref,
    scale_ref, edge_v, sum_v, grams_ref,
):
    core = lax.axis_index("col")
    ny, nx = mask_ref.shape[2:]
    half = near_ref.shape[2] // 2
    n = 2 * half
    root = jnp.sqrt(lookup(material_ref[3 * core], table_ref))
    for comp in range(3):
        scale_ref[comp] = mask_ref[comp, 3 * core].astype(F32) / root
    scale_ref[2] = scale_ref[2] * core.astype(F32)
    edge_v[...] = jnp.zeros_like(edge_v)
    for halo_ref, side in ((halo_own_ref, core), (halo_other_ref, 1 - core)):
        for group in range(half // GROUP):
            row = pl.multiple_of(side * half + group * GROUP, GROUP)
            from_ = pl.ds(group * GROUP, GROUP)
            h1_last = None
            for y in range(ny):
                h0 = halo_ref[0, y, from_, :]
                h1 = halo_ref[1, y, from_, :]
                change = (h0, h1, minus(h1_last, h1) + behind_x(h0))
                for comp in range(3):
                    value = near_ref[comp, y, pl.ds(row, GROUP), :] - change[comp] * scale_ref[comp, y : y + 1, :]
                    put_v(edge_v, row, comp, y, ny, value)
                h1_last = h1
    sum_v[...] = acc_v_ref[...]
    dots_uv(edge_u_ref, edge_v, sum_v, half)
    cross = sum_v[0:n, 0:n]
    grams_ref[2] = sum_v[0:n, 128 : 128 + n] + (cross + cross.T)
    cross = acc_u_ref[:, n : 2 * n]
    grams_ref[1] = acc_u_ref[:, 0:n] + (cross + cross.T)
    rows = sum_v[n : 2 * n, :] + sum_v[2 * n : 3 * n, :]
    grams_ref[0] = rows[:, 0:n] + rows[:, 128 : 128 + n]
    for side, out_ref in ((core, keep_rows_ref), (1 - core, send_rows_ref)):
        at = pl.ds(pl.multiple_of(side * half, 8), half)
        out_ref[...] = pack(core, side == 1, grams_ref.at[0], grams_ref.at[1], grams_ref.at[2], at, half)


def finish(near, halo_own, halo_other, mask, material, table, edge_u, acc_v, acc_u):
    _, ny, n, nx = near.shape
    total = edge_u.shape[0]
    rows = jax.ShapeDtypeStruct((n // 2, 256), F32)
    return pl.pallas_call(
        finish_kernel,
        out_shape=(rows, rows),
        in_specs=[VMEM, VMEM, VMEM, VMEM, VMEM, SMEM, VMEM, VMEM, VMEM],
        out_specs=[VMEM, VMEM],
        scratch_shapes=[
            pltpu.VMEM((3, ny, nx), F32),
            pltpu.VMEM((total, 256, LANES), BF16),
            pltpu.VMEM(acc_v.shape, F32),
            pltpu.VMEM((3, n, n), F32),
        ],
        compiler_params=pltpu.CompilerParams(vmem_limit_bytes=36 * MIB),
    )(near, halo_own, halo_other, mask, material, table, edge_u, acc_v, acc_u)


def ahead(field, axis):
    size = field.shape[axis]
    at = lax.broadcasted_iota(jnp.int32, field.shape, axis)
    return jnp.where(at == size - 1, 0.0, pltpu.roll(field, size - 1, axis)) - field


def behind(field, axis):
    at = lax.broadcasted_iota(jnp.int32, field.shape, axis)
    return jnp.where(at == 0, 0.0, pltpu.roll(field, 1, axis)) - field


def image_kernel(first, block_ref, one_ref, two_ref, mask_ref, image_ref, keep_ref):
    upper = lax.axis_index("col") == 1
    ncol, _, nz, ny, nx = block_ref.shape
    keep_ref[...] = mask_ref[...].astype(F32)
    ones = one_ref.reshape(2 * ny * ncol, nx)
    twos = two_ref.reshape(2 * ny * ncol, nx)

    def body(j, carry):
        col = first + j

        def e(comp, layer):
            return block_ref[col, comp, layer] * keep_ref[comp, layer]

        at0 = pl.ds(col, ny, stride=ncol)
        at1 = pl.ds(ny * ncol + col, ny, stride=ncol)
        one0, one1, two0, two1 = ones[at0, :], ones[at1, :], twos[at0, :], twos[at1, :]
        x, y, z = (e(comp, 0) for comp in range(3))
        lowy = x - jnp.where(upper, two0, one0)
        lowx = jnp.where(upper, two1, one1) - y
        for layer in range(nz):
            if layer + 1 < nz:
                xn, yn, zn = (e(comp, layer + 1) for comp in range(3))
            else:
                xn, yn, zn = jnp.where(upper, one0, two0), jnp.where(upper, one1, two1), None
            topx = ahead(z, 0) - (yn - y)
            topy = (xn - x) - ahead(z, 1)
            hz = ahead(y, 1) - ahead(x, 0)
            image_ref[j, 0, layer] = ((lowy - topy) - behind(hz, 0)) * keep_ref[0, layer]
            image_ref[j, 1, layer] = (behind(hz, 1) - (lowx - topx)) * keep_ref[1, layer]
            image_ref[j, 2, layer] = (behind(topx, 0) - behind(topy, 1)) * keep_ref[2, layer]
            x, y, z, lowx, lowy = xn, yn, zn, topx, topy
        return carry

    lax.fori_loop(0, image_ref.shape[0], body, 0, unroll=4)


def image_of(block, one, two, mask, first, count):
    _, _, nz, ny, nx = block.shape
    return pl.pallas_call(
        functools.partial(image_kernel, first),
        out_shape=jax.ShapeDtypeStruct((count,) + block.shape[1:], F32),
        in_specs=[VMEM] * 4,
        out_specs=VMEM,
        scratch_shapes=[pltpu.VMEM((3, nz, ny, nx), F32)],
        compiler_params=pltpu.CompilerParams(vmem_limit_bytes=16 * MIB),
        cost_estimate=pl.CostEstimate(flops=10**7, bytes_accessed=3 * 10**6, transcendentals=0),
    )(block, one, two, mask)


PARTS = 4
PIECES = 8


def residual_kernel(
    scale, rows_ref, block_ref, image0_ref, image1_ref, image2_ref, image3_ref, mask_ref, material_ref, table_ref,
    out_ref, ga_ref, gb_ref, gf_ref, mass_ref, theta_ref, buffer, sems,
):
    swap = lax.axis_index("col") == 1
    half, total = ga_ref.shape
    down = lax.broadcasted_iota(jnp.int32, (half, half), 0)
    across = lax.broadcasted_iota(jnp.int32, (half, half), 1)
    rows = rows_ref[...] * scale
    mixed, fa, ab, bb, fb = (rows[:, k * half : (k + 1) * half] for k in range(5))
    diag_b = rows[:, 5 * half : 5 * half + 1]
    diag_a = jnp.sum(jnp.where(down == across, mixed, 0.0), axis=1, keepdims=True)
    theta_ref[...] = jnp.broadcast_to(diag_a / diag_b, theta_ref.shape)
    mass_ref[...] = lookup(material_ref[...], table_ref)[None] * mask_ref[...].astype(F32)
    ncol = block_ref.shape[0]
    per = ncol // PIECES
    images = (image0_ref, image1_ref, image2_ref, image3_ref)
    copies = []
    for piece in range(PIECES):
        part, start = divmod(piece * per, ncol // PARTS)
        for j in range(per):
            col = piece * per + j
            theta = theta_ref[col : col + 1, :]
            buffer[col] = images[part][start + j] - theta[None, None] * (mass_ref[...] * block_ref[col])
        some = pl.ds(piece * per, per)
        copies.append(pltpu.make_async_copy(buffer.at[some], out_ref.at[some], sems.at[piece]))
        copies[-1].start()
    flat = mixed.T
    aa = jnp.where(across <= down, mixed, flat)
    ba = jnp.where(across == down, diag_b, jnp.where(across > down, mixed, flat))
    for ref, a, b in ((ga_ref, aa, ab), (gb_ref, ba, bb), (gf_ref, fa, fb)):
        ref[...] = jnp.concatenate([jnp.where(swap, b, a), jnp.where(swap, a, b)], axis=1)
    for copy in copies:
        copy.wait()


def residual_of(rows, block, images, mask, material, table, scale):
    ncol, _, nz, ny, nx = block.shape
    gram = jax.ShapeDtypeStruct((ncol, 2 * ncol), F32)
    return pl.pallas_call(
        functools.partial(residual_kernel, scale),
        out_shape=(jax.ShapeDtypeStruct(block.shape, F32), gram, gram, gram),
        in_specs=[VMEM] * (PARTS + 4) + [SMEM],
        out_specs=[HBM] + [VMEM] * 3,
        scratch_shapes=[
            pltpu.VMEM((3, nz, ny, nx), F32),
            pltpu.VMEM((ncol, nx), F32),
            pltpu.VMEM(block.shape, F32),
            pltpu.SemaphoreType.DMA((PIECES,)),
        ],
        compiler_params=pltpu.CompilerParams(vmem_limit_bytes=24 * MIB),
        cost_estimate=pl.CostEstimate(flops=2 * 10**7, bytes_accessed=15 * 10**6, transcendentals=0),
    )(rows, block, *images, mask, material, table)


def exchange_rounds(slabs):
    nz, ny, nx = GRIDS[slabs]
    rounds = []
    for size, stride in ((nx, 1), (ny, nx), (nz, nx * ny)):
        for flip in {2: (1,), 4: (1, 3), 8: (1, 2, 7)}[size]:
            rounds.append([i + ((i // stride % size) ^ flip) * stride - i // stride % size * stride for i in range(slabs)])
    shift = {2: 1, 8: 3}[nz]
    turned = rounds[-shift:] + rounds[:-shift]
    return [
        [(2 * i, 2 * a[i]) for i in range(slabs)] + [(2 * i + 1, 2 * b[i] + 1) for i in range(slabs)]
        for a, b in zip(rounds, turned)
    ]


def shards(block, material, table, mask):
    slabs = lax.axis_size("space")
    ncol, _, nz, ny, nx = block.shape
    scale = 1.0 / (3.0 * nz * slabs * ny * nx)
    swap = [(0, 1), (1, 0)]
    both = ("space", "col")
    other = lax.ppermute(block, "col", swap)
    one, two = edges(block, mask)
    straight = [(2 * i, 2 * i + 2) for i in range(slabs - 1)] + [(2 * i + 3, 2 * i + 1) for i in range(slabs - 1)]
    crossed = [(2 * i + 1, 2 * i + 2) for i in range(slabs - 1)] + [(2 * i + 2, 2 * i + 1) for i in range(slabs - 1)]
    halo_own = lax.ppermute(one, both, straight)
    halo_other = lax.ppermute(two, both, crossed)
    near, edge_u, acc_v, acc_u = middle(block, other, mask, material, table)
    keep_rows, send_rows = finish(near, halo_own, halo_other, mask, material, table, edge_u, acc_v, acc_u)
    rows = keep_rows + lax.ppermute(send_rows, "col", swap)
    rows, halo_other = lax.optimization_barrier((rows, halo_other))
    halo_far = lax.ppermute(halo_other, "col", swap)
    images = []
    for index, pairs in enumerate(exchange_rounds(slabs)):
        arrived = lax.ppermute(rows, both, pairs)
        if 1 <= index <= PARTS:
            held, halo_far = lax.optimization_barrier((rows, halo_far))
            count = ncol // PARTS
            image = image_of(block, halo_own, halo_far, mask, (index - 1) * count, count)
            arrived, image = lax.optimization_barrier((arrived, image))
            images.append(image)
        rows = rows + arrived
    return residual_of(rows, block, images, mask, material, table, scale)


def solution(mesh):
    in_specs = (
        P("col", None, "space", None, None),
        P("space", None, None),
        P(),
        P(None, "space", None, None),
    )
    out_specs = (
        P("col", None, "space", None, None),
        P("col", None),
        P("col", None),
        P("col", None),
    )
    return jax.shard_map(shards, mesh=mesh, in_specs=in_specs, out_specs=out_specs, check_vma=False)
```

```python
import functools

import jax
import jax.numpy as jnp
from jax import lax
from jax.experimental import pallas as pl
from jax.experimental.pallas import tpu as pltpu
from jax.sharding import PartitionSpec as P

MIB = 1 << 20
GRIDS = {128: (8, 4, 4), 8: (2, 2, 2)}
F32 = jnp.float32
BF16 = jnp.bfloat16
NT = (((1,), (1,)), ((), ()))
VMEM = pl.BlockSpec(memory_space=pltpu.VMEM)
SMEM = pl.BlockSpec(memory_space=pltpu.SMEM)
HBM = pl.BlockSpec(memory_space=pltpu.HBM)
GROUP = 16
LANES = 512
EDGE_LIMIT = 51
OWN_LIMIT = 48
OTHER_LIMIT = 30


def lookup(material, table_ref):
    eps = jnp.zeros(material.shape, F32)
    for index in range(table_ref.shape[0]):
        eps = jnp.where(material == index, table_ref[index], eps)
    return eps


def split(value):
    high = value.astype(BF16)
    return high, (value - high.astype(F32)).astype(BF16)


def ahead_x(field):
    at = lax.broadcasted_iota(jnp.int32, field.shape, 1)
    size = field.shape[1]
    return jnp.where(at == size - 1, 0.0, pltpu.roll(field, size - 1, 1)) - field


def behind_x(field):
    at = lax.broadcasted_iota(jnp.int32, field.shape, 1)
    return jnp.where(at == 0, 0.0, pltpu.roll(field, 1, 1)) - field


def minus(left, right):
    return -right if left is None else left - right


def edges_kernel(block_ref, mask_ref, one_ref, two_ref, first_ref, last_ref, mask_first, mask_last, sems):
    ncol, _, nz, ny, nx = block_ref.shape
    groups = ncol // GROUP
    masks = [
        pltpu.make_async_copy(mask_ref.at[0:2, 0], mask_first, sems.at[0]),
        pltpu.make_async_copy(mask_ref.at[:, nz - 1], mask_last, sems.at[1]),
    ]
    for copy in masks:
        copy.start()
    copies = []
    for group in range(groups):
        some = pl.ds(group * GROUP, GROUP)
        copies.append((
            pltpu.make_async_copy(block_ref.at[some, 0:2, 0], first_ref.at[some], sems.at[2 + 2 * group]),
            pltpu.make_async_copy(block_ref.at[some, :, nz - 1], last_ref.at[some], sems.at[3 + 2 * group]),
        ))
        for copy in copies[-1]:
            copy.start()
    for copy in masks:
        copy.wait()
    swap = lax.axis_index("col") == 1
    slab = lax.axis_index("space")
    lowest = (slab != 0).astype(F32)
    highest = (slab != lax.axis_size("space") - 1).astype(F32)
    first = first_ref.reshape(ncol * 2 * ny, nx)
    last = last_ref.reshape(ncol * 3 * ny, nx)
    for group in range(groups):
        for copy in copies[group]:
            copy.wait()
        out = pl.ds(group * GROUP, GROUP)

        def low(comp, y):
            keep = mask_first[comp, y : y + 1, :].astype(F32) * lowest
            return first[pl.ds((group * GROUP * 2 + comp) * ny + y, GROUP, stride=2 * ny), :] * keep

        def high(comp, y):
            keep = mask_last[comp, y : y + 1, :].astype(F32) * highest
            return last[pl.ds((group * GROUP * 3 + comp) * ny + y, GROUP, stride=3 * ny), :] * keep

        ez = high(2, 0)
        for y in range(ny):
            ez_next = high(2, y + 1) if y + 1 < ny else None
            up0 = high(0, y) + ahead_x(ez)
            up1 = high(1, y) + minus(ez_next, ez)
            down0 = low(0, y)
            down1 = low(1, y)
            one_ref[0, y, out, :] = jnp.where(swap, down0, up0)
            one_ref[1, y, out, :] = jnp.where(swap, down1, up1)
            two_ref[0, y, out, :] = jnp.where(swap, up0, down0)
            two_ref[1, y, out, :] = jnp.where(swap, up1, down1)
            ez = ez_next


def edges(block, mask):
    ncol, _, nz, ny, nx = block.shape
    shape = jax.ShapeDtypeStruct((2, ny, ncol, nx), F32)
    return pl.pallas_call(
        edges_kernel,
        out_shape=(shape, shape),
        in_specs=[HBM, HBM],
        out_specs=[VMEM, VMEM],
        scratch_shapes=[
            pltpu.VMEM((ncol, 2, ny, nx), F32),
            pltpu.VMEM((ncol, 3, ny, nx), F32),
            pltpu.VMEM((2, ny, nx), jnp.int32),
            pltpu.VMEM((3, ny, nx), jnp.int32),
            pltpu.SemaphoreType.DMA((2 + 2 * (ncol // GROUP),)),
        ],
        compiler_params=pltpu.CompilerParams(vmem_limit_bytes=EDGE_LIMIT * MIB),
    )(block, mask)


def place(comp, y, ny, nx):
    at = (comp * ny + y) * nx
    return at // LANES, pl.ds(at % LANES, nx)


def put(ref, row, comp, y, ny, value):
    at, lanes = place(comp, y, ny, value.shape[1])
    high, low = split(value)
    ref[at, pl.ds(row, GROUP), lanes] = high
    ref[at, pl.ds(ref.shape[1] // 2 + row, GROUP), lanes] = low


def parts(first_ref, second_ref, k):
    half = first_ref.shape[1] // 2
    high = jnp.concatenate([first_ref[k, 0:half, :], second_ref[k, 0:half, :]], axis=0)
    low = jnp.concatenate([first_ref[k, half : 2 * half, :], second_ref[k, half : 2 * half, :]], axis=0)
    return high, low


def dots_uv(us, vs, acc_ref):
    def step(k, carry):
        v_high, v_low = parts(*vs, k)
        left = jnp.concatenate([v_high, *parts(*us, k)], axis=0)
        right = jnp.concatenate([v_low, v_high], axis=0)
        acc_ref[...] += lax.dot_general(left, right, NT, preferred_element_type=F32)
        return carry

    lax.fori_loop(0, us[0].shape[0], step, 0, unroll=6)


def dots_uu(us, acc_ref):
    def step(k, carry):
        high, low = parts(*us, k)
        right = jnp.concatenate([high, low], axis=0)
        acc_ref[...] += lax.dot_general(high, right, NT, preferred_element_type=F32)
        return carry

    lax.fori_loop(0, us[0].shape[0], step, 0, unroll=6)


def start_window(src_ref, window_ref, sems):
    copies = []
    for group in range(src_ref.shape[0] // GROUP):
        some = pl.ds(group * GROUP, GROUP)
        layers = pl.ds(lax.axis_index("col"), 3)
        copies.append(pltpu.make_async_copy(src_ref.at[some, :, layers], window_ref.at[some], sems.at[group]))
        copies[-1].start()
    return copies


def maps(mask_ref, material_ref, table_ref, keep_ref, scale_ref, root_ref):
    core = lax.axis_index("col")
    for place_, layer in enumerate((core + 1, 3 * core)):
        root = jnp.sqrt(lookup(material_ref[layer], table_ref))
        root_ref[place_] = root
        for comp in range(3):
            scale_ref[place_, comp] = mask_ref[comp, layer].astype(F32) / root
    for layer in range(3):
        for comp in range(3):
            keep_ref[comp, layer] = mask_ref[comp, core + layer].astype(F32)


def ahead(field, axis):
    size = field.shape[axis]
    at = lax.broadcasted_iota(jnp.int32, field.shape, axis)
    return jnp.where(at == size - 1, 0.0, pltpu.roll(field, size - 1, axis)) - field


def behind(field, axis):
    at = lax.broadcasted_iota(jnp.int32, field.shape, axis)
    return jnp.where(at == 0, 0.0, pltpu.roll(field, 1, axis)) - field


UNROLL = 4


def columns(copies, window_ref, base, keep_ref, scale_ref, root_ref, tmp_ref, near_ref, edge_u, mid_u, mid_v):
    upper = lax.axis_index("col") == 1
    ny, nx = window_ref.shape[3:]
    for group in range(window_ref.shape[0] // GROUP):
        if copies:
            copies[group].wait()

        def body(j, carry):
            def e(comp, layer):
                return window_ref[group * GROUP + j, comp, base + layer] * keep_ref[comp, layer]

            rows = pl.ds(pl.multiple_of(j * ny, ny), ny)

            def store(kind, values):
                for comp, value in enumerate(values):
                    tmp_ref[kind, comp, rows, :] = value

            x0, y0, z0 = (e(comp, 0) for comp in range(3))
            x1, y1, z1 = (e(comp, 1) for comp in range(3))
            x2, y2, z2 = (e(comp, 2) for comp in range(3))
            h01x = ahead(z0, 0) - (y1 - y0)
            h01y = (x1 - x0) - ahead(z0, 1)
            h12x = ahead(z1, 0) - (y2 - y1)
            h12y = (x2 - x1) - ahead(z1, 1)
            h1z = ahead(y1, 1) - ahead(x1, 0)
            store(0, (
                ((h01y - h12y) - behind(h1z, 0)) * scale_ref[0, 0],
                (behind(h1z, 1) - (h01x - h12x)) * scale_ref[0, 1],
                (behind(h12x, 0) - behind(h12y, 1)) * scale_ref[0, 2],
            ))
            store(1, (value * root_ref[0] for value in (x1, y1, z1)))
            xb, yb, zb = (jnp.where(upper, up, low) for up, low in ((x2, x0), (y2, y0), (z2, z0)))
            hbz = ahead(yb, 1) - ahead(xb, 0)
            lowx = jnp.where(upper, h12x, -yb)
            lowy = jnp.where(upper, h12y, xb)
            topx = jnp.where(upper, ahead(zb, 0) + yb, h01x)
            topy = jnp.where(upper, -xb - ahead(zb, 1), h01y)
            store(2, (
                ((lowy - topy) - behind(hbz, 0)) * scale_ref[1, 0],
                (behind(hbz, 1) - (lowx - topx)) * scale_ref[1, 1],
                (behind(topx, 0) - behind(topy, 1)) * scale_ref[1, 2],
            ))
            store(3, (value * root_ref[1] for value in (xb, yb, zb)))
            return carry

        lax.fori_loop(0, GROUP, body, 0, unroll=UNROLL)
        row = group * GROUP
        for comp in range(3):
            for y in range(ny):
                v, u, near, edge = (tmp_ref[kind, comp, pl.ds(y, GROUP, stride=ny), :] for kind in range(4))
                put(mid_v, row, comp, y, ny, v)
                put(mid_u, row, comp, y, ny, u)
                near_ref[comp, y, pl.ds(row, GROUP), :] = near
                put(edge_u, row, comp, y, ny, edge)


def mine_kernel(
    src_ref, mask_ref, material_ref, table_ref,
    near_ref, edge_u, mid_u, mid_v, mass_ref, window_ref, keep_ref, scale_ref, root_ref, tmp_ref, sems,
):
    copies = start_window(src_ref, window_ref, sems)
    maps(mask_ref, material_ref, table_ref, keep_ref, scale_ref, root_ref)
    mass_ref[...] = mask_ref[...].astype(F32) * lookup(material_ref[...], table_ref)[None]
    columns(copies, window_ref, 0, keep_ref, scale_ref, root_ref, tmp_ref, near_ref, edge_u, mid_u, mid_v)


def theirs_kernel(
    src_ref, mask_ref, material_ref, table_ref, own_edge_u, own_mid_u, own_mid_v,
    near_ref, edge_u, acc_v_ref, acc_u_ref, keep_ref, scale_ref, root_ref, tmp_ref, mid_u, mid_v,
):
    maps(mask_ref, material_ref, table_ref, keep_ref, scale_ref, root_ref)
    acc_v_ref[...] = jnp.zeros_like(acc_v_ref)
    acc_u_ref[...] = jnp.zeros_like(acc_u_ref)
    columns(None, src_ref, lax.axis_index("col"), keep_ref, scale_ref, root_ref, tmp_ref, near_ref, edge_u, mid_u, mid_v)
    dots_uv((own_mid_u, mid_u), (own_mid_v, mid_v), acc_v_ref)
    dots_uu((own_mid_u, mid_u), acc_u_ref)
    dots_uu((own_edge_u, edge_u), acc_u_ref)


def common(block, mask):
    ncol, _, nz, ny, nx = block.shape
    near = jax.ShapeDtypeStruct((3, ny, ncol, nx), F32)
    operand = jax.ShapeDtypeStruct((3 * ny * nx // LANES, 2 * ncol, LANES), BF16)
    scratch = [
        pltpu.VMEM((ncol, 3, 3, ny, nx), F32),
        pltpu.VMEM((3, 3, ny, nx), F32),
        pltpu.VMEM((2, 3, ny, nx), F32),
        pltpu.VMEM((2, ny, nx), F32),
        pltpu.VMEM((4, 3, GROUP * ny, nx), F32),
    ]
    return near, operand, scratch, pltpu.SemaphoreType.DMA((ncol // GROUP,))


def mine(block, mask, material, table):
    near, operand, scratch, sems = common(block, mask)
    return pl.pallas_call(
        mine_kernel,
        out_shape=(near, operand, operand, operand, jax.ShapeDtypeStruct(mask.shape, F32)),
        in_specs=[HBM, VMEM, VMEM, SMEM],
        out_specs=[VMEM] * 5,
        scratch_shapes=scratch + [sems],
        compiler_params=pltpu.CompilerParams(vmem_limit_bytes=OWN_LIMIT * MIB),
        cost_estimate=pl.CostEstimate(flops=10**8, bytes_accessed=8 * 10**6, transcendentals=0),
    )(block, mask, material, table)


def theirs(other, mask, material, table, own_edge_u, own_mid_u, own_mid_v):
    ncol = other.shape[0]
    near, operand, scratch, _ = common(other, mask)
    return pl.pallas_call(
        theirs_kernel,
        out_shape=(
            near, operand,
            jax.ShapeDtypeStruct((6 * ncol, 4 * ncol), F32),
            jax.ShapeDtypeStruct((2 * ncol, 4 * ncol), F32),
        ),
        in_specs=[VMEM, VMEM, VMEM, SMEM, VMEM, VMEM, VMEM],
        out_specs=[VMEM] * 4,
        scratch_shapes=scratch[1:] + [pltpu.VMEM(operand.shape, BF16), pltpu.VMEM(operand.shape, BF16)],
        compiler_params=pltpu.CompilerParams(vmem_limit_bytes=OTHER_LIMIT * MIB),
        cost_estimate=pl.CostEstimate(flops=2 * 10**9, bytes_accessed=8 * 10**6, transcendentals=0),
    )(other, mask, material, table, own_edge_u, own_mid_u, own_mid_v)


def pack(ga, gb, gf, side, half):
    rows = slice(side * half, (side + 1) * half)
    near = slice(side * half, (side + 1) * half)
    far = slice((1 - side) * half, (2 - side) * half)
    down = lax.broadcasted_iota(jnp.int32, (half, half), 0)
    across = lax.broadcasted_iota(jnp.int32, (half, half), 1)
    aa, ba, fa = (gram[rows, near] for gram in (ga, gb, gf))
    diag = jnp.sum(jnp.where(down == across, ba, 0.0), axis=1, keepdims=True)
    mixed = jnp.where(across <= down, aa, ba)
    wide = jnp.broadcast_to(diag, (half, 256 - 5 * half))
    return jnp.concatenate([mixed, fa, ga[rows, far], gb[rows, far], gf[rows, far], wide], axis=1)


def halo_rows(near_ref, halo_ref, mask_ref, material_ref, table_ref, scale_ref, out_ref):
    core = lax.axis_index("col")
    ny, nx = mask_ref.shape[2:]
    half = near_ref.shape[2]
    root = jnp.sqrt(lookup(material_ref[3 * core], table_ref))
    for comp in range(3):
        scale_ref[comp] = mask_ref[comp, 3 * core].astype(F32) / root
    scale_ref[2] = scale_ref[2] * core.astype(F32)
    for group in range(half // GROUP):
        row = group * GROUP
        rows = pl.ds(row, GROUP)
        h1_last = None
        for y in range(ny):
            h0 = halo_ref[0, y, rows, :]
            h1 = halo_ref[1, y, rows, :]
            change = (h0, h1, minus(h1_last, h1) + behind_x(h0))
            for comp in range(3):
                value = near_ref[comp, y, rows, :] - change[comp] * scale_ref[comp, y : y + 1, :]
                put(out_ref, row, comp, y, ny, value)
            h1_last = h1


def own_kernel(near_ref, halo_ref, mask_ref, material_ref, table_ref, out_ref, scale_ref):
    halo_rows(near_ref, halo_ref, mask_ref, material_ref, table_ref, scale_ref, out_ref)


def own_rows(near, halo, mask, material, table):
    _, ny, half, nx = near.shape
    return pl.pallas_call(
        own_kernel,
        out_shape=jax.ShapeDtypeStruct((3 * ny * nx // LANES, 2 * half, LANES), BF16),
        in_specs=[VMEM, VMEM, VMEM, VMEM, SMEM],
        out_specs=VMEM,
        scratch_shapes=[pltpu.VMEM((3, ny, nx), F32)],
        compiler_params=pltpu.CompilerParams(vmem_limit_bytes=16 * MIB),
        cost_estimate=pl.CostEstimate(flops=10**7, bytes_accessed=10**6, transcendentals=0),
    )(near, halo, mask, material, table)


def finish_kernel(
    near_ref, halo_ref, mask_ref, material_ref, table_ref, own_v, own_u, other_u, acc_v_ref, acc_u_ref,
    keep_rows_ref, send_rows_ref, scale_ref, other_v, sum_v,
):
    half = near_ref.shape[2]
    n = 2 * half
    halo_rows(near_ref, halo_ref, mask_ref, material_ref, table_ref, scale_ref, other_v)
    sum_v[...] = acc_v_ref[...]
    dots_uv((own_u, other_u), (own_v, other_v), sum_v)
    cross = sum_v[0:n, 0:n]
    gf = sum_v[0:n, n : 2 * n] + (cross + cross.T)
    cross = acc_u_ref[:, n : 2 * n]
    gb = acc_u_ref[:, 0:n] + (cross + cross.T)
    rows = sum_v[n : 2 * n, :] + sum_v[2 * n : 3 * n, :]
    ga = rows[:, 0:n] + rows[:, n : 2 * n]
    keep_rows_ref[...] = pack(ga, gb, gf, 0, half)
    send_rows_ref[...] = pack(ga, gb, gf, 1, half)


def finish(near, halo, mask, material, table, own_v, own_u, other_u, acc_v, acc_u):
    _, ny, half, nx = near.shape
    rows = jax.ShapeDtypeStruct((half, 256), F32)
    return pl.pallas_call(
        finish_kernel,
        out_shape=(rows, rows),
        in_specs=[VMEM, VMEM, VMEM, VMEM, SMEM] + [VMEM] * 5,
        out_specs=[VMEM, VMEM],
        scratch_shapes=[
            pltpu.VMEM((3, ny, nx), F32),
            pltpu.VMEM(own_v.shape, BF16),
            pltpu.VMEM(acc_v.shape, F32),
        ],
        compiler_params=pltpu.CompilerParams(vmem_limit_bytes=24 * MIB),
    )(near, halo, mask, material, table, own_v, own_u, other_u, acc_v, acc_u)


def image_kernel(first, block_ref, one_ref, two_ref, mask_ref, image_ref, keep_ref):
    upper = lax.axis_index("col") == 1
    ncol, _, nz, ny, nx = block_ref.shape
    keep_ref[...] = mask_ref[...].astype(F32)
    ones = one_ref.reshape(2 * ny * ncol, nx)
    twos = two_ref.reshape(2 * ny * ncol, nx)

    def body(j, carry):
        col = first + j

        def e(comp, layer):
            return block_ref[col, comp, layer] * keep_ref[comp, layer]

        at0 = pl.ds(col, ny, stride=ncol)
        at1 = pl.ds(ny * ncol + col, ny, stride=ncol)
        one0, one1, two0, two1 = ones[at0, :], ones[at1, :], twos[at0, :], twos[at1, :]
        x, y, z = (e(comp, 0) for comp in range(3))
        lowy = x - jnp.where(upper, two0, one0)
        lowx = jnp.where(upper, two1, one1) - y
        for layer in range(nz):
            if layer + 1 < nz:
                xn, yn, zn = (e(comp, layer + 1) for comp in range(3))
            else:
                xn, yn, zn = jnp.where(upper, one0, two0), jnp.where(upper, one1, two1), None
            topx = ahead(z, 0) - (yn - y)
            topy = (xn - x) - ahead(z, 1)
            hz = ahead(y, 1) - ahead(x, 0)
            image_ref[j, 0, layer] = ((lowy - topy) - behind(hz, 0)) * keep_ref[0, layer]
            image_ref[j, 1, layer] = (behind(hz, 1) - (lowx - topx)) * keep_ref[1, layer]
            image_ref[j, 2, layer] = (behind(topx, 0) - behind(topy, 1)) * keep_ref[2, layer]
            x, y, z, lowx, lowy = xn, yn, zn, topx, topy
        return carry

    lax.fori_loop(0, image_ref.shape[0], body, 0, unroll=4)


def image_of(block, one, two, mask, first, count):
    _, _, nz, ny, nx = block.shape
    return pl.pallas_call(
        functools.partial(image_kernel, first),
        out_shape=jax.ShapeDtypeStruct((count,) + block.shape[1:], F32),
        in_specs=[VMEM] * 4,
        out_specs=VMEM,
        scratch_shapes=[pltpu.VMEM((3, nz, ny, nx), F32)],
        compiler_params=pltpu.CompilerParams(vmem_limit_bytes=16 * MIB),
        cost_estimate=pl.CostEstimate(flops=10**7, bytes_accessed=3 * 10**6, transcendentals=0),
    )(block, one, two, mask)


PARTS = 3
PIECES = 12


def residual_kernel(
    scale, rows_ref, block_ref, image0_ref, image1_ref, image2_ref, mass_ref,
    out_ref, ga_ref, gb_ref, gf_ref, theta_ref, buffer, sems,
):
    swap = lax.axis_index("col") == 1
    half, total = ga_ref.shape
    down = lax.broadcasted_iota(jnp.int32, (half, half), 0)
    across = lax.broadcasted_iota(jnp.int32, (half, half), 1)
    rows = rows_ref[...] * scale
    mixed, fa, ab, bb, fb = (rows[:, k * half : (k + 1) * half] for k in range(5))
    diag_b = rows[:, 5 * half : 5 * half + 1]
    diag_a = jnp.sum(jnp.where(down == across, mixed, 0.0), axis=1, keepdims=True)
    theta_ref[...] = jnp.broadcast_to(diag_a / diag_b, theta_ref.shape)
    ncol = block_ref.shape[0]
    per = ncol // PIECES
    images = (image0_ref, image1_ref, image2_ref)
    copies = []
    for piece in range(PIECES):
        part, start = divmod(piece * per, ncol // PARTS)
        for j in range(per):
            col = piece * per + j
            theta = theta_ref[col : col + 1, :]
            buffer[col] = images[part][start + j] - theta[None, None] * (mass_ref[...] * block_ref[col])
        some = pl.ds(piece * per, per)
        copies.append(pltpu.make_async_copy(buffer.at[some], out_ref.at[some], sems.at[piece]))
        copies[-1].start()
    flat = mixed.T
    aa = jnp.where(across <= down, mixed, flat)
    ba = jnp.where(across == down, diag_b, jnp.where(across > down, mixed, flat))
    for ref, a, b in ((ga_ref, aa, ab), (gb_ref, ba, bb), (gf_ref, fa, fb)):
        ref[...] = jnp.concatenate([jnp.where(swap, b, a), jnp.where(swap, a, b)], axis=1)
    for copy in copies:
        copy.wait()


def residual_of(rows, block, images, mass, scale):
    ncol, _, nz, ny, nx = block.shape
    gram = jax.ShapeDtypeStruct((ncol, 2 * ncol), F32)
    return pl.pallas_call(
        functools.partial(residual_kernel, scale),
        out_shape=(jax.ShapeDtypeStruct(block.shape, F32), gram, gram, gram),
        in_specs=[VMEM] * (PARTS + 3),
        out_specs=[HBM] + [VMEM] * 3,
        scratch_shapes=[
            pltpu.VMEM((ncol, nx), F32),
            pltpu.VMEM(block.shape, F32),
            pltpu.SemaphoreType.DMA((PIECES,)),
        ],
        compiler_params=pltpu.CompilerParams(vmem_limit_bytes=24 * MIB),
        cost_estimate=pl.CostEstimate(flops=2 * 10**7, bytes_accessed=15 * 10**6, transcendentals=0),
    )(rows, block, *images, mass)


def exchange_rounds(slabs):
    nz, ny, nx = GRIDS[slabs]

    def partners(size, stride, flip):
        return [i + ((i // stride % size) ^ flip) * stride - i // stride % size * stride for i in range(slabs)]

    def flips(size):
        return (1, 2, 3) if size >= 4 else (1,)

    x, y, z = ([partners(size, stride, flip) for flip in flips(size)] for size, stride in ((nx, 1), (ny, nx), (nz, nx * ny)))
    stages = [(x, y), (y, x), (z, z)]
    if nz == 8:
        halves = [partners(nz, nx * ny, 7)]
        stages.append((halves, halves))
    return [
        [
            [(2 * i, 2 * a[i]) for i in range(slabs)] + [(2 * i + 1, 2 * b[i] + 1) for i in range(slabs)]
            for a, b in zip(first, second)
        ]
        for first, second in stages
    ]


def shards(block, material, table, mask):
    slabs = lax.axis_size("space")
    ncol, _, nz, ny, nx = block.shape
    scale = 1.0 / (3.0 * nz * slabs * ny * nx)
    swap = [(0, 1), (1, 0)]
    both = ("space", "col")
    other = lax.ppermute(block, "col", swap)
    one, two = edges(block, mask)
    straight = [pair for i in range(slabs) for pair in ((2 * i, 2 * ((i + 1) % slabs)), (2 * ((i + 1) % slabs) + 1, 2 * i + 1))]
    crossed = [pair for i in range(slabs) for pair in ((2 * i + 1, 2 * ((i + 1) % slabs)), (2 * ((i + 1) % slabs), 2 * i + 1))]
    halo_own = lax.ppermute(one, both, straight)
    halo_other = lax.ppermute(two, both, crossed)
    near_own, own_u, *mid, mass = mine(block, mask, material, table)
    near_other, other_u, acc_v, acc_u = theirs(other, mask, material, table, own_u, *mid)
    near_own, near_other, halo_own, halo_other = lax.optimization_barrier((near_own, near_other, halo_own, halo_other))
    own_v = own_rows(near_own, halo_own, mask, material, table)
    keep_rows, send_rows = finish(near_other, halo_other, mask, material, table, own_v, own_u, other_u, acc_v, acc_u)
    rows = keep_rows + lax.ppermute(send_rows, "col", swap)
    rows, halo_other = lax.optimization_barrier((rows, halo_other))
    halo_far = lax.ppermute(halo_other, "col", swap)
    images = []
    for index, stage in enumerate(exchange_rounds(slabs)):
        arrived = [lax.ppermute(rows, both, pairs) for pairs in stage]
        if index >= 1:
            rows, halo_far = lax.optimization_barrier((rows, halo_far))
            count = ncol // PARTS
            image = image_of(block, halo_own, halo_far, mask, (index - 1) * count, count)
            arrived, image = lax.optimization_barrier((arrived, image))
            images.append(image)
        rows = rows + arrived[0]
        if len(arrived) == 3:
            rows = rows + (arrived[1] + arrived[2])
    return residual_of(rows, block, images, mass, scale)


def solution(mesh):
    in_specs = (
        P("col", None, "space", None, None),
        P("space", None, None),
        P(),
        P(None, "space", None, None),
    )
    out_specs = (
        P("col", None, "space", None, None),
        P("col", None),
        P("col", None),
        P("col", None),
    )
    return jax.shard_map(shards, mesh=mesh, in_specs=in_specs, out_specs=out_specs, check_vma=False)
```

```python
import functools

import jax
import jax.numpy as jnp
from jax import lax
from jax.experimental import pallas as pl
from jax.experimental.pallas import tpu as pltpu
from jax.sharding import PartitionSpec as P

MIB = 1 << 20
GRIDS = {128: (8, 4, 4), 8: (2, 2, 2)}
F32 = jnp.float32
BF16 = jnp.bfloat16
NT = (((1,), (1,)), ((), ()))
VMEM = pl.BlockSpec(memory_space=pltpu.VMEM)
SMEM = pl.BlockSpec(memory_space=pltpu.SMEM)
HBM = pl.BlockSpec(memory_space=pltpu.HBM)
GROUP = 16
LANES = 512
EDGE_LIMIT = 51
OWN_LIMIT = 48
OTHER_LIMIT = 30


def lookup(material, table_ref):
    eps = jnp.zeros(material.shape, F32)
    for index in range(table_ref.shape[0]):
        eps = jnp.where(material == index, table_ref[index], eps)
    return eps


def split(value):
    high = value.astype(BF16)
    return high, (value - high.astype(F32)).astype(BF16)


def ahead_x(field):
    at = lax.broadcasted_iota(jnp.int32, field.shape, 1)
    size = field.shape[1]
    return jnp.where(at == size - 1, 0.0, pltpu.roll(field, size - 1, 1)) - field


def behind_x(field):
    at = lax.broadcasted_iota(jnp.int32, field.shape, 1)
    return jnp.where(at == 0, 0.0, pltpu.roll(field, 1, 1)) - field


def minus(left, right):
    return -right if left is None else left - right


def edges_kernel(block_ref, mask_ref, one_ref, two_ref, first_ref, last_ref, mask_first, mask_last, sems):
    ncol, _, nz, ny, nx = block_ref.shape
    groups = ncol // GROUP
    masks = [
        pltpu.make_async_copy(mask_ref.at[0:2, 0], mask_first, sems.at[0]),
        pltpu.make_async_copy(mask_ref.at[:, nz - 1], mask_last, sems.at[1]),
    ]
    for copy in masks:
        copy.start()
    copies = []
    for group in range(groups):
        some = pl.ds(group * GROUP, GROUP)
        copies.append((
            pltpu.make_async_copy(block_ref.at[some, 0:2, 0], first_ref.at[some], sems.at[2 + 2 * group]),
            pltpu.make_async_copy(block_ref.at[some, :, nz - 1], last_ref.at[some], sems.at[3 + 2 * group]),
        ))
        for copy in copies[-1]:
            copy.start()
    for copy in masks:
        copy.wait()
    swap = lax.axis_index("col") == 1
    slab = lax.axis_index("space")
    lowest = (slab != 0).astype(F32)
    highest = (slab != lax.axis_size("space") - 1).astype(F32)
    first = first_ref.reshape(ncol * 2 * ny, nx)
    last = last_ref.reshape(ncol * 3 * ny, nx)
    for group in range(groups):
        for copy in copies[group]:
            copy.wait()
        out = pl.ds(group * GROUP, GROUP)

        def low(comp, y):
            keep = mask_first[comp, y : y + 1, :].astype(F32) * lowest
            return first[pl.ds((group * GROUP * 2 + comp) * ny + y, GROUP, stride=2 * ny), :] * keep

        def high(comp, y):
            keep = mask_last[comp, y : y + 1, :].astype(F32) * highest
            return last[pl.ds((group * GROUP * 3 + comp) * ny + y, GROUP, stride=3 * ny), :] * keep

        ez = high(2, 0)
        for y in range(ny):
            ez_next = high(2, y + 1) if y + 1 < ny else None
            up0 = high(0, y) + ahead_x(ez)
            up1 = high(1, y) + minus(ez_next, ez)
            down0 = low(0, y)
            down1 = low(1, y)
            one_ref[0, y, out, :] = jnp.where(swap, down0, up0)
            one_ref[1, y, out, :] = jnp.where(swap, down1, up1)
            two_ref[0, y, out, :] = jnp.where(swap, up0, down0)
            two_ref[1, y, out, :] = jnp.where(swap, up1, down1)
            ez = ez_next


def edges(block, mask):
    ncol, _, nz, ny, nx = block.shape
    shape = jax.ShapeDtypeStruct((2, ny, ncol, nx), F32)
    return pl.pallas_call(
        edges_kernel,
        out_shape=(shape, shape),
        in_specs=[HBM, HBM],
        out_specs=[VMEM, VMEM],
        scratch_shapes=[
            pltpu.VMEM((ncol, 2, ny, nx), F32),
            pltpu.VMEM((ncol, 3, ny, nx), F32),
            pltpu.VMEM((2, ny, nx), jnp.int32),
            pltpu.VMEM((3, ny, nx), jnp.int32),
            pltpu.SemaphoreType.DMA((2 + 2 * (ncol // GROUP),)),
        ],
        compiler_params=pltpu.CompilerParams(vmem_limit_bytes=EDGE_LIMIT * MIB),
    )(block, mask)


def place(comp, y, ny, nx):
    at = (comp * ny + y) * nx
    return at // LANES, pl.ds(at % LANES, nx)


def put(ref, row, comp, y, ny, value):
    at, lanes = place(comp, y, ny, value.shape[1])
    high, low = split(value)
    ref[at, pl.ds(row, GROUP), lanes] = high
    ref[at, pl.ds(ref.shape[1] // 2 + row, GROUP), lanes] = low


def parts(first_ref, second_ref, k):
    half = first_ref.shape[1] // 2
    high = jnp.concatenate([first_ref[k, 0:half, :], second_ref[k, 0:half, :]], axis=0)
    low = jnp.concatenate([first_ref[k, half : 2 * half, :], second_ref[k, half : 2 * half, :]], axis=0)
    return high, low


def dots_uv(us, vs, acc_ref):
    def step(k, carry):
        v_high, v_low = parts(*vs, k)
        left = jnp.concatenate([v_high, *parts(*us, k)], axis=0)
        right = jnp.concatenate([v_low, v_high], axis=0)
        acc_ref[...] += lax.dot_general(left, right, NT, preferred_element_type=F32)
        return carry

    lax.fori_loop(0, us[0].shape[0], step, 0, unroll=6)


def dots_uu(us, acc_ref):
    def step(k, carry):
        high, low = parts(*us, k)
        right = jnp.concatenate([high, low], axis=0)
        acc_ref[...] += lax.dot_general(high, right, NT, preferred_element_type=F32)
        return carry

    lax.fori_loop(0, us[0].shape[0], step, 0, unroll=6)


def start_window(src_ref, window_ref, sems):
    copies = []
    for group in range(src_ref.shape[0] // GROUP):
        some = pl.ds(group * GROUP, GROUP)
        layers = pl.ds(lax.axis_index("col"), 3)
        copies.append(pltpu.make_async_copy(src_ref.at[some, :, layers], window_ref.at[some], sems.at[group]))
        copies[-1].start()
    return copies


def maps(mask_ref, material_ref, table_ref, keep_ref, scale_ref, root_ref):
    core = lax.axis_index("col")
    for place_, layer in enumerate((core + 1, 3 * core)):
        root = jnp.sqrt(lookup(material_ref[layer], table_ref))
        root_ref[place_] = root
        for comp in range(3):
            scale_ref[place_, comp] = mask_ref[comp, layer].astype(F32) / root
    for layer in range(3):
        for comp in range(3):
            keep_ref[comp, layer] = mask_ref[comp, core + layer].astype(F32)


def ahead(field, axis):
    size = field.shape[axis]
    at = lax.broadcasted_iota(jnp.int32, field.shape, axis)
    return jnp.where(at == size - 1, 0.0, pltpu.roll(field, size - 1, axis)) - field


def behind(field, axis):
    at = lax.broadcasted_iota(jnp.int32, field.shape, axis)
    return jnp.where(at == 0, 0.0, pltpu.roll(field, 1, axis)) - field


UNROLL = 4


def columns(copies, window_ref, base, keep_ref, scale_ref, root_ref, tmp_ref, near_ref, edge_u, mid_u, mid_v):
    upper = lax.axis_index("col") == 1
    ny, nx = window_ref.shape[3:]
    for group in range(window_ref.shape[0] // GROUP):
        if copies:
            copies[group].wait()

        def body(j, carry):
            def e(comp, layer):
                return window_ref[group * GROUP + j, comp, base + layer] * keep_ref[comp, layer]

            rows = pl.ds(pl.multiple_of(j * ny, ny), ny)

            def store(kind, values):
                for comp, value in enumerate(values):
                    tmp_ref[kind, comp, rows, :] = value

            x0, y0, z0 = (e(comp, 0) for comp in range(3))
            x1, y1, z1 = (e(comp, 1) for comp in range(3))
            x2, y2, z2 = (e(comp, 2) for comp in range(3))
            h01x = ahead(z0, 0) - (y1 - y0)
            h01y = (x1 - x0) - ahead(z0, 1)
            h12x = ahead(z1, 0) - (y2 - y1)
            h12y = (x2 - x1) - ahead(z1, 1)
            h1z = ahead(y1, 1) - ahead(x1, 0)
            store(0, (
                ((h01y - h12y) - behind(h1z, 0)) * scale_ref[0, 0],
                (behind(h1z, 1) - (h01x - h12x)) * scale_ref[0, 1],
                (behind(h12x, 0) - behind(h12y, 1)) * scale_ref[0, 2],
            ))
            store(1, (value * root_ref[0] for value in (x1, y1, z1)))
            xb, yb, zb = (jnp.where(upper, up, low) for up, low in ((x2, x0), (y2, y0), (z2, z0)))
            hbz = ahead(yb, 1) - ahead(xb, 0)
            lowx = jnp.where(upper, h12x, -yb)
            lowy = jnp.where(upper, h12y, xb)
            topx = jnp.where(upper, ahead(zb, 0) + yb, h01x)
            topy = jnp.where(upper, -xb - ahead(zb, 1), h01y)
            store(2, (
                ((lowy - topy) - behind(hbz, 0)) * scale_ref[1, 0],
                (behind(hbz, 1) - (lowx - topx)) * scale_ref[1, 1],
                (behind(topx, 0) - behind(topy, 1)) * scale_ref[1, 2],
            ))
            store(3, (value * root_ref[1] for value in (xb, yb, zb)))
            return carry

        lax.fori_loop(0, GROUP, body, 0, unroll=UNROLL)
        row = group * GROUP
        for comp in range(3):
            for y in range(ny):
                v, u, near, edge = (tmp_ref[kind, comp, pl.ds(y, GROUP, stride=ny), :] for kind in range(4))
                put(mid_v, row, comp, y, ny, v)
                put(mid_u, row, comp, y, ny, u)
                near_ref[comp, y, pl.ds(row, GROUP), :] = near
                put(edge_u, row, comp, y, ny, edge)


def mine_kernel(
    src_ref, mask_ref, material_ref, table_ref,
    near_ref, edge_u, mid_u, mid_v, mass_ref, window_ref, keep_ref, scale_ref, root_ref, tmp_ref, sems,
):
    copies = start_window(src_ref, window_ref, sems)
    maps(mask_ref, material_ref, table_ref, keep_ref, scale_ref, root_ref)
    mass_ref[...] = mask_ref[...].astype(F32) * lookup(material_ref[...], table_ref)[None]
    columns(copies, window_ref, 0, keep_ref, scale_ref, root_ref, tmp_ref, near_ref, edge_u, mid_u, mid_v)


def theirs_kernel(
    src_ref, mask_ref, material_ref, table_ref, own_edge_u, own_mid_u, own_mid_v,
    near_ref, edge_u, acc_v_ref, acc_u_ref, keep_ref, scale_ref, root_ref, tmp_ref, mid_u, mid_v,
):
    maps(mask_ref, material_ref, table_ref, keep_ref, scale_ref, root_ref)
    acc_v_ref[...] = jnp.zeros_like(acc_v_ref)
    acc_u_ref[...] = jnp.zeros_like(acc_u_ref)
    columns(None, src_ref, lax.axis_index("col"), keep_ref, scale_ref, root_ref, tmp_ref, near_ref, edge_u, mid_u, mid_v)
    dots_uv((own_mid_u, mid_u), (own_mid_v, mid_v), acc_v_ref)
    dots_uu((own_mid_u, mid_u), acc_u_ref)
    dots_uu((own_edge_u, edge_u), acc_u_ref)


def common(block, mask):
    ncol, _, nz, ny, nx = block.shape
    near = jax.ShapeDtypeStruct((3, ny, ncol, nx), F32)
    operand = jax.ShapeDtypeStruct((3 * ny * nx // LANES, 2 * ncol, LANES), BF16)
    scratch = [
        pltpu.VMEM((ncol, 3, 3, ny, nx), F32),
        pltpu.VMEM((3, 3, ny, nx), F32),
        pltpu.VMEM((2, 3, ny, nx), F32),
        pltpu.VMEM((2, ny, nx), F32),
        pltpu.VMEM((4, 3, GROUP * ny, nx), F32),
    ]
    return near, operand, scratch, pltpu.SemaphoreType.DMA((ncol // GROUP,))


def mine(block, mask, material, table):
    near, operand, scratch, sems = common(block, mask)
    return pl.pallas_call(
        mine_kernel,
        out_shape=(near, operand, operand, operand, jax.ShapeDtypeStruct(mask.shape, F32)),
        in_specs=[HBM, VMEM, VMEM, SMEM],
        out_specs=[VMEM] * 5,
        scratch_shapes=scratch + [sems],
        compiler_params=pltpu.CompilerParams(vmem_limit_bytes=OWN_LIMIT * MIB),
        cost_estimate=pl.CostEstimate(flops=10**8, bytes_accessed=8 * 10**6, transcendentals=0),
    )(block, mask, material, table)


def theirs(other, mask, material, table, own_edge_u, own_mid_u, own_mid_v):
    ncol = other.shape[0]
    near, operand, scratch, _ = common(other, mask)
    return pl.pallas_call(
        theirs_kernel,
        out_shape=(
            near, operand,
            jax.ShapeDtypeStruct((6 * ncol, 4 * ncol), F32),
            jax.ShapeDtypeStruct((2 * ncol, 4 * ncol), F32),
        ),
        in_specs=[VMEM, VMEM, VMEM, SMEM, VMEM, VMEM, VMEM],
        out_specs=[VMEM] * 4,
        scratch_shapes=scratch[1:] + [pltpu.VMEM(operand.shape, BF16), pltpu.VMEM(operand.shape, BF16)],
        compiler_params=pltpu.CompilerParams(vmem_limit_bytes=OTHER_LIMIT * MIB),
        cost_estimate=pl.CostEstimate(flops=2 * 10**9, bytes_accessed=8 * 10**6, transcendentals=0),
    )(other, mask, material, table, own_edge_u, own_mid_u, own_mid_v)


def pack(ga, gb, gf, side, half):
    rows = slice(side * half, (side + 1) * half)
    near = slice(side * half, (side + 1) * half)
    far = slice((1 - side) * half, (2 - side) * half)
    down = lax.broadcasted_iota(jnp.int32, (half, half), 0)
    across = lax.broadcasted_iota(jnp.int32, (half, half), 1)
    aa, ba, fa = (gram[rows, near] for gram in (ga, gb, gf))
    diag = jnp.sum(jnp.where(down == across, ba, 0.0), axis=1, keepdims=True)
    mixed = jnp.where(across <= down, aa, ba)
    wide = jnp.broadcast_to(diag, (half, 256 - 5 * half))
    return jnp.concatenate([mixed, fa, ga[rows, far], gb[rows, far], gf[rows, far], wide], axis=1)


def halo_rows(near_ref, halo_ref, mask_ref, material_ref, table_ref, scale_ref, out_ref):
    core = lax.axis_index("col")
    ny, nx = mask_ref.shape[2:]
    half = near_ref.shape[2]
    root = jnp.sqrt(lookup(material_ref[3 * core], table_ref))
    for comp in range(3):
        scale_ref[comp] = mask_ref[comp, 3 * core].astype(F32) / root
    scale_ref[2] = scale_ref[2] * core.astype(F32)
    for group in range(half // GROUP):
        row = group * GROUP
        rows = pl.ds(row, GROUP)
        h1_last = None
        for y in range(ny):
            h0 = halo_ref[0, y, rows, :]
            h1 = halo_ref[1, y, rows, :]
            change = (h0, h1, minus(h1_last, h1) + behind_x(h0))
            for comp in range(3):
                value = near_ref[comp, y, rows, :] - change[comp] * scale_ref[comp, y : y + 1, :]
                put(out_ref, row, comp, y, ny, value)
            h1_last = h1


def own_kernel(near_ref, halo_ref, mask_ref, material_ref, table_ref, out_ref, scale_ref):
    halo_rows(near_ref, halo_ref, mask_ref, material_ref, table_ref, scale_ref, out_ref)


def own_rows(near, halo, mask, material, table):
    _, ny, half, nx = near.shape
    return pl.pallas_call(
        own_kernel,
        out_shape=jax.ShapeDtypeStruct((3 * ny * nx // LANES, 2 * half, LANES), BF16),
        in_specs=[VMEM, VMEM, VMEM, VMEM, SMEM],
        out_specs=VMEM,
        scratch_shapes=[pltpu.VMEM((3, ny, nx), F32)],
        compiler_params=pltpu.CompilerParams(vmem_limit_bytes=16 * MIB),
        cost_estimate=pl.CostEstimate(flops=10**7, bytes_accessed=10**6, transcendentals=0),
    )(near, halo, mask, material, table)


def finish_kernel(
    near_ref, halo_ref, mask_ref, material_ref, table_ref, own_v, own_u, other_u, acc_v_ref, acc_u_ref,
    keep_rows_ref, send_rows_ref, scale_ref, other_v, sum_v,
):
    half = near_ref.shape[2]
    n = 2 * half
    halo_rows(near_ref, halo_ref, mask_ref, material_ref, table_ref, scale_ref, other_v)
    sum_v[...] = acc_v_ref[...]
    dots_uv((own_u, other_u), (own_v, other_v), sum_v)
    cross = sum_v[0:n, 0:n]
    gf = sum_v[0:n, n : 2 * n] + (cross + cross.T)
    cross = acc_u_ref[:, n : 2 * n]
    gb = acc_u_ref[:, 0:n] + (cross + cross.T)
    rows = sum_v[n : 2 * n, :] + sum_v[2 * n : 3 * n, :]
    ga = rows[:, 0:n] + rows[:, n : 2 * n]
    keep_rows_ref[...] = pack(ga, gb, gf, 0, half)
    send_rows_ref[...] = pack(ga, gb, gf, 1, half)


def finish(near, halo, mask, material, table, own_v, own_u, other_u, acc_v, acc_u):
    _, ny, half, nx = near.shape
    rows = jax.ShapeDtypeStruct((half, 256), F32)
    return pl.pallas_call(
        finish_kernel,
        out_shape=(rows, rows),
        in_specs=[VMEM, VMEM, VMEM, VMEM, SMEM] + [VMEM] * 5,
        out_specs=[VMEM, VMEM],
        scratch_shapes=[
            pltpu.VMEM((3, ny, nx), F32),
            pltpu.VMEM(own_v.shape, BF16),
            pltpu.VMEM(acc_v.shape, F32),
        ],
        compiler_params=pltpu.CompilerParams(vmem_limit_bytes=24 * MIB),
    )(near, halo, mask, material, table, own_v, own_u, other_u, acc_v, acc_u)


def image_kernel(first, block_ref, one_ref, two_ref, mask_ref, image_ref, keep_ref):
    upper = lax.axis_index("col") == 1
    ncol, _, nz, ny, nx = block_ref.shape
    keep_ref[...] = mask_ref[...].astype(F32)
    ones = one_ref.reshape(2 * ny * ncol, nx)
    twos = two_ref.reshape(2 * ny * ncol, nx)

    def body(j, carry):
        col = first + j

        def e(comp, layer):
            return block_ref[col, comp, layer] * keep_ref[comp, layer]

        at0 = pl.ds(col, ny, stride=ncol)
        at1 = pl.ds(ny * ncol + col, ny, stride=ncol)
        one0, one1, two0, two1 = ones[at0, :], ones[at1, :], twos[at0, :], twos[at1, :]
        x, y, z = (e(comp, 0) for comp in range(3))
        lowy = x - jnp.where(upper, two0, one0)
        lowx = jnp.where(upper, two1, one1) - y
        for layer in range(nz):
            if layer + 1 < nz:
                xn, yn, zn = (e(comp, layer + 1) for comp in range(3))
            else:
                xn, yn, zn = jnp.where(upper, one0, two0), jnp.where(upper, one1, two1), None
            topx = ahead(z, 0) - (yn - y)
            topy = (xn - x) - ahead(z, 1)
            hz = ahead(y, 1) - ahead(x, 0)
            image_ref[j, 0, layer] = ((lowy - topy) - behind(hz, 0)) * keep_ref[0, layer]
            image_ref[j, 1, layer] = (behind(hz, 1) - (lowx - topx)) * keep_ref[1, layer]
            image_ref[j, 2, layer] = (behind(topx, 0) - behind(topy, 1)) * keep_ref[2, layer]
            x, y, z, lowx, lowy = xn, yn, zn, topx, topy
        return carry

    lax.fori_loop(0, image_ref.shape[0], body, 0, unroll=4)


def image_of(block, one, two, mask, first, count):
    _, _, nz, ny, nx = block.shape
    return pl.pallas_call(
        functools.partial(image_kernel, first),
        out_shape=jax.ShapeDtypeStruct((count,) + block.shape[1:], F32),
        in_specs=[VMEM] * 4,
        out_specs=VMEM,
        scratch_shapes=[pltpu.VMEM((3, nz, ny, nx), F32)],
        compiler_params=pltpu.CompilerParams(vmem_limit_bytes=16 * MIB),
        cost_estimate=pl.CostEstimate(flops=10**7, bytes_accessed=3 * 10**6, transcendentals=0),
    )(block, one, two, mask)


PARTS = 3
PIECES = 12


def residual_kernel(
    scale, rows_ref, block_ref, image0_ref, image1_ref, image2_ref, mass_ref,
    out_ref, ga_ref, gb_ref, gf_ref, theta_ref, buffer, sems,
):
    swap = lax.axis_index("col") == 1
    half, total = ga_ref.shape
    down = lax.broadcasted_iota(jnp.int32, (half, half), 0)
    across = lax.broadcasted_iota(jnp.int32, (half, half), 1)
    rows = rows_ref[...] * scale
    mixed, fa, ab, bb, fb = (rows[:, k * half : (k + 1) * half] for k in range(5))
    diag_b = rows[:, 5 * half : 5 * half + 1]
    diag_a = jnp.sum(jnp.where(down == across, mixed, 0.0), axis=1, keepdims=True)
    theta_ref[...] = jnp.broadcast_to(diag_a / diag_b, theta_ref.shape)
    ncol = block_ref.shape[0]
    per = ncol // PIECES
    images = (image0_ref, image1_ref, image2_ref)
    copies = []
    for piece in range(PIECES):
        part, start = divmod(piece * per, ncol // PARTS)
        for j in range(per):
            col = piece * per + j
            theta = theta_ref[col : col + 1, :]
            buffer[col] = images[part][start + j] - theta[None, None] * (mass_ref[...] * block_ref[col])
        some = pl.ds(piece * per, per)
        copies.append(pltpu.make_async_copy(buffer.at[some], out_ref.at[some], sems.at[piece]))
        copies[-1].start()
    flat = mixed.T
    aa = jnp.where(across <= down, mixed, flat)
    ba = jnp.where(across == down, diag_b, jnp.where(across > down, mixed, flat))
    for ref, a, b in ((ga_ref, aa, ab), (gb_ref, ba, bb), (gf_ref, fa, fb)):
        ref[...] = jnp.concatenate([jnp.where(swap, b, a), jnp.where(swap, a, b)], axis=1)
    for copy in copies:
        copy.wait()


def residual_of(rows, block, images, mass, scale):
    ncol, _, nz, ny, nx = block.shape
    gram = jax.ShapeDtypeStruct((ncol, 2 * ncol), F32)
    return pl.pallas_call(
        functools.partial(residual_kernel, scale),
        out_shape=(jax.ShapeDtypeStruct(block.shape, F32), gram, gram, gram),
        in_specs=[VMEM] * (PARTS + 3),
        out_specs=[HBM] + [VMEM] * 3,
        scratch_shapes=[
            pltpu.VMEM((ncol, nx), F32),
            pltpu.VMEM(block.shape, F32),
            pltpu.SemaphoreType.DMA((PIECES,)),
        ],
        compiler_params=pltpu.CompilerParams(vmem_limit_bytes=24 * MIB),
        cost_estimate=pl.CostEstimate(flops=2 * 10**7, bytes_accessed=15 * 10**6, transcendentals=0),
    )(rows, block, *images, mass)


def exchange_rounds(slabs):
    nz, ny, nx = GRIDS[slabs]

    def partners(size, stride, flip):
        return [i + ((i // stride % size) ^ flip) * stride - i // stride % size * stride for i in range(slabs)]

    def stage(first, second, flips):
        exchanges = {}
        for flip in flips:
            a, b = (partners(size, stride, flip) for size, stride in (first, second))
            exchanges[flip] = [(2 * i, 2 * a[i]) for i in range(slabs)] + [(2 * i + 1, 2 * b[i] + 1) for i in range(slabs)]
        return exchanges

    x, y, z = (nx, 1), (ny, nx), (nz, nx * ny)
    if nx < 4:
        return [stage(x, y, (1,)), stage(y, x, (1,)), stage(z, z, (1,))]
    return [stage(x, y, (3, 2, 1)), stage(y, x, (2, 1, 3)), stage(z, z, (3, 2, 1)), stage(z, z, (7,))]


def shards(block, material, table, mask):
    slabs = lax.axis_size("space")
    ncol, _, nz, ny, nx = block.shape
    scale = 1.0 / (3.0 * nz * slabs * ny * nx)
    swap = [(0, 1), (1, 0)]
    both = ("space", "col")
    other = lax.ppermute(block, "col", swap)
    one, two = edges(block, mask)
    straight = [pair for i in range(slabs) for pair in ((2 * i, 2 * ((i + 1) % slabs)), (2 * ((i + 1) % slabs) + 1, 2 * i + 1))]
    crossed = [pair for i in range(slabs) for pair in ((2 * i + 1, 2 * ((i + 1) % slabs)), (2 * ((i + 1) % slabs), 2 * i + 1))]
    halo_own = lax.ppermute(one, both, straight)
    halo_other = lax.ppermute(two, both, crossed)
    near_own, own_u, *mid, mass = mine(block, mask, material, table)
    near_other, other_u, acc_v, acc_u = theirs(other, mask, material, table, own_u, *mid)
    near_own, near_other, halo_own = lax.optimization_barrier((near_own, near_other, halo_own))
    own_v = own_rows(near_own, halo_own, mask, material, table)
    keep_rows, send_rows = finish(near_other, halo_other, mask, material, table, own_v, own_u, other_u, acc_v, acc_u)
    rows = keep_rows + lax.ppermute(send_rows, "col", swap)
    rows, halo_other = lax.optimization_barrier((rows, halo_other))
    halo_far = lax.ppermute(halo_other, "col", swap)
    images = []
    for index, stage in enumerate(exchange_rounds(slabs)):
        arrived = {flip: lax.ppermute(rows, both, pairs) for flip, pairs in stage.items()}
        if index >= 1:
            rows, halo_far = lax.optimization_barrier((rows, halo_far))
            count = ncol // PARTS
            image = image_of(block, halo_own, halo_far, mask, (index - 1) * count, count)
            arrived, image = lax.optimization_barrier((arrived, image))
            images.append(image)
        rows = rows + (arrived[1] if 1 in arrived else arrived[7])
        if len(arrived) == 3:
            rows = rows + (arrived[2] + arrived[3])
    return residual_of(rows, block, images, mass, scale)


def solution(mesh):
    in_specs = (
        P("col", None, "space", None, None),
        P("space", None, None),
        P(),
        P(None, "space", None, None),
    )
    out_specs = (
        P("col", None, "space", None, None),
        P("col", None),
        P("col", None),
        P("col", None),
    )
    return jax.shard_map(shards, mesh=mesh, in_specs=in_specs, out_specs=out_specs, check_vma=False)
```

```python
import functools

import jax
import jax.numpy as jnp
from jax import lax
from jax.experimental import pallas as pl
from jax.experimental.pallas import tpu as pltpu
from jax.sharding import PartitionSpec as P

MIB = 1 << 20
GRIDS = {128: (8, 4, 4), 8: (2, 2, 2)}
F32 = jnp.float32
BF16 = jnp.bfloat16
NT = (((1,), (1,)), ((), ()))
VMEM = pl.BlockSpec(memory_space=pltpu.VMEM)
SMEM = pl.BlockSpec(memory_space=pltpu.SMEM)
HBM = pl.BlockSpec(memory_space=pltpu.HBM)
GROUP = 16
LANES = 512
EDGE_LIMIT = 51
OWN_LIMIT = 48
OTHER_LIMIT = 30


def lookup(material, table_ref):
    eps = jnp.zeros(material.shape, F32)
    for index in range(table_ref.shape[0]):
        eps = jnp.where(material == index, table_ref[index], eps)
    return eps


def split(value):
    high = value.astype(BF16)
    return high, (value - high.astype(F32)).astype(BF16)


def ahead_x(field):
    at = lax.broadcasted_iota(jnp.int32, field.shape, 1)
    size = field.shape[1]
    return jnp.where(at == size - 1, 0.0, pltpu.roll(field, size - 1, 1)) - field


def behind_x(field):
    at = lax.broadcasted_iota(jnp.int32, field.shape, 1)
    return jnp.where(at == 0, 0.0, pltpu.roll(field, 1, 1)) - field


def minus(left, right):
    return -right if left is None else left - right


def edges_kernel(block_ref, mask_ref, one_ref, two_ref, first_ref, last_ref, mask_first, mask_last, sems):
    ncol, _, nz, ny, nx = block_ref.shape
    groups = ncol // GROUP
    masks = [
        pltpu.make_async_copy(mask_ref.at[0:2, 0], mask_first, sems.at[0]),
        pltpu.make_async_copy(mask_ref.at[:, nz - 1], mask_last, sems.at[1]),
    ]
    for copy in masks:
        copy.start()
    copies = []
    for group in range(groups):
        some = pl.ds(group * GROUP, GROUP)
        copies.append((
            pltpu.make_async_copy(block_ref.at[some, 0:2, 0], first_ref.at[some], sems.at[2 + 2 * group]),
            pltpu.make_async_copy(block_ref.at[some, :, nz - 1], last_ref.at[some], sems.at[3 + 2 * group]),
        ))
        for copy in copies[-1]:
            copy.start()
    for copy in masks:
        copy.wait()
    swap = lax.axis_index("col") == 1
    slab = lax.axis_index("space")
    lowest = (slab != 0).astype(F32)
    highest = (slab != lax.axis_size("space") - 1).astype(F32)
    first = first_ref.reshape(ncol * 2 * ny, nx)
    last = last_ref.reshape(ncol * 3 * ny, nx)
    for group in range(groups):
        for copy in copies[group]:
            copy.wait()
        out = pl.ds(group * GROUP, GROUP)

        def low(comp, y):
            keep = mask_first[comp, y : y + 1, :].astype(F32) * lowest
            return first[pl.ds((group * GROUP * 2 + comp) * ny + y, GROUP, stride=2 * ny), :] * keep

        def high(comp, y):
            keep = mask_last[comp, y : y + 1, :].astype(F32) * highest
            return last[pl.ds((group * GROUP * 3 + comp) * ny + y, GROUP, stride=3 * ny), :] * keep

        ez = high(2, 0)
        for y in range(ny):
            ez_next = high(2, y + 1) if y + 1 < ny else None
            up0 = high(0, y) + ahead_x(ez)
            up1 = high(1, y) + minus(ez_next, ez)
            down0 = low(0, y)
            down1 = low(1, y)
            one_ref[0, y, out, :] = jnp.where(swap, down0, up0)
            one_ref[1, y, out, :] = jnp.where(swap, down1, up1)
            two_ref[0, y, out, :] = jnp.where(swap, up0, down0)
            two_ref[1, y, out, :] = jnp.where(swap, up1, down1)
            ez = ez_next


def edges(block, mask):
    ncol, _, nz, ny, nx = block.shape
    shape = jax.ShapeDtypeStruct((2, ny, ncol, nx), F32)
    return pl.pallas_call(
        edges_kernel,
        out_shape=(shape, shape),
        in_specs=[HBM, HBM],
        out_specs=[VMEM, VMEM],
        scratch_shapes=[
            pltpu.VMEM((ncol, 2, ny, nx), F32),
            pltpu.VMEM((ncol, 3, ny, nx), F32),
            pltpu.VMEM((2, ny, nx), jnp.int32),
            pltpu.VMEM((3, ny, nx), jnp.int32),
            pltpu.SemaphoreType.DMA((2 + 2 * (ncol // GROUP),)),
        ],
        compiler_params=pltpu.CompilerParams(vmem_limit_bytes=EDGE_LIMIT * MIB),
    )(block, mask)


def place(comp, y, ny, nx):
    at = (comp * ny + y) * nx
    return at // LANES, pl.ds(at % LANES, nx)


def put(ref, row, comp, y, ny, value):
    at, lanes = place(comp, y, ny, value.shape[1])
    high, low = split(value)
    ref[at, pl.ds(row, GROUP), lanes] = high
    ref[at, pl.ds(ref.shape[1] // 2 + row, GROUP), lanes] = low


def parts(first_ref, second_ref, k):
    half = first_ref.shape[1] // 2
    high = jnp.concatenate([first_ref[k, 0:half, :], second_ref[k, 0:half, :]], axis=0)
    low = jnp.concatenate([first_ref[k, half : 2 * half, :], second_ref[k, half : 2 * half, :]], axis=0)
    return high, low


def dots_uv(us, vs, acc_ref):
    def step(k, carry):
        v_high, v_low = parts(*vs, k)
        left = jnp.concatenate([v_high, *parts(*us, k)], axis=0)
        right = jnp.concatenate([v_low, v_high], axis=0)
        acc_ref[...] += lax.dot_general(left, right, NT, preferred_element_type=F32)
        return carry

    lax.fori_loop(0, us[0].shape[0], step, 0, unroll=6)


def dots_uu(us, acc_ref):
    def step(k, carry):
        high, low = parts(*us, k)
        right = jnp.concatenate([high, low], axis=0)
        acc_ref[...] += lax.dot_general(high, right, NT, preferred_element_type=F32)
        return carry

    lax.fori_loop(0, us[0].shape[0], step, 0, unroll=6)


def start_window(src_ref, window_ref, sems):
    copies = []
    for group in range(src_ref.shape[0] // GROUP):
        some = pl.ds(group * GROUP, GROUP)
        layers = pl.ds(lax.axis_index("col"), 3)
        copies.append(pltpu.make_async_copy(src_ref.at[some, :, layers], window_ref.at[some], sems.at[group]))
        copies[-1].start()
    return copies


def maps(mask_ref, material_ref, table_ref, keep_ref, scale_ref, root_ref):
    core = lax.axis_index("col")
    for place_, layer in enumerate((core + 1, 3 * core)):
        root = jnp.sqrt(lookup(material_ref[layer], table_ref))
        root_ref[place_] = root
        for comp in range(3):
            scale_ref[place_, comp] = mask_ref[comp, layer].astype(F32) / root
    for layer in range(3):
        for comp in range(3):
            keep_ref[comp, layer] = mask_ref[comp, core + layer].astype(F32)


def ahead(field, axis):
    size = field.shape[axis]
    at = lax.broadcasted_iota(jnp.int32, field.shape, axis)
    return jnp.where(at == size - 1, 0.0, pltpu.roll(field, size - 1, axis)) - field


def behind(field, axis):
    at = lax.broadcasted_iota(jnp.int32, field.shape, axis)
    return jnp.where(at == 0, 0.0, pltpu.roll(field, 1, axis)) - field


UNROLL = 4


def columns(copies, window_ref, base, keep_ref, scale_ref, root_ref, tmp_ref, near_ref, edge_u, mid_u, mid_v):
    upper = lax.axis_index("col") == 1
    ny, nx = window_ref.shape[3:]
    for group in range(window_ref.shape[0] // GROUP):
        if copies:
            copies[group].wait()

        def body(j, carry):
            def e(comp, layer):
                return window_ref[group * GROUP + j, comp, base + layer] * keep_ref[comp, layer]

            rows = pl.ds(pl.multiple_of(j * ny, ny), ny)

            def store(kind, values):
                for comp, value in enumerate(values):
                    tmp_ref[kind, comp, rows, :] = value

            x0, y0, z0 = (e(comp, 0) for comp in range(3))
            x1, y1, z1 = (e(comp, 1) for comp in range(3))
            x2, y2, z2 = (e(comp, 2) for comp in range(3))
            h01x = ahead(z0, 0) - (y1 - y0)
            h01y = (x1 - x0) - ahead(z0, 1)
            h12x = ahead(z1, 0) - (y2 - y1)
            h12y = (x2 - x1) - ahead(z1, 1)
            h1z = ahead(y1, 1) - ahead(x1, 0)
            store(0, (
                ((h01y - h12y) - behind(h1z, 0)) * scale_ref[0, 0],
                (behind(h1z, 1) - (h01x - h12x)) * scale_ref[0, 1],
                (behind(h12x, 0) - behind(h12y, 1)) * scale_ref[0, 2],
            ))
            store(1, (value * root_ref[0] for value in (x1, y1, z1)))
            xb, yb, zb = (jnp.where(upper, up, low) for up, low in ((x2, x0), (y2, y0), (z2, z0)))
            hbz = ahead(yb, 1) - ahead(xb, 0)
            lowx = jnp.where(upper, h12x, -yb)
            lowy = jnp.where(upper, h12y, xb)
            topx = jnp.where(upper, ahead(zb, 0) + yb, h01x)
            topy = jnp.where(upper, -xb - ahead(zb, 1), h01y)
            store(2, (
                ((lowy - topy) - behind(hbz, 0)) * scale_ref[1, 0],
                (behind(hbz, 1) - (lowx - topx)) * scale_ref[1, 1],
                (behind(topx, 0) - behind(topy, 1)) * scale_ref[1, 2],
            ))
            store(3, (value * root_ref[1] for value in (xb, yb, zb)))
            return carry

        lax.fori_loop(0, GROUP, body, 0, unroll=UNROLL)
        row = group * GROUP
        for comp in range(3):
            for y in range(ny):
                v, u, near, edge = (tmp_ref[kind, comp, pl.ds(y, GROUP, stride=ny), :] for kind in range(4))
                put(mid_v, row, comp, y, ny, v)
                put(mid_u, row, comp, y, ny, u)
                near_ref[comp, y, pl.ds(row, GROUP), :] = near
                put(edge_u, row, comp, y, ny, edge)


def mine_kernel(
    src_ref, mask_ref, material_ref, table_ref,
    near_ref, edge_u, mid_u, mid_v, mass_ref, window_ref, keep_ref, scale_ref, root_ref, tmp_ref, sems,
):
    copies = start_window(src_ref, window_ref, sems)
    maps(mask_ref, material_ref, table_ref, keep_ref, scale_ref, root_ref)
    mass_ref[...] = mask_ref[...].astype(F32) * lookup(material_ref[...], table_ref)[None]
    columns(copies, window_ref, 0, keep_ref, scale_ref, root_ref, tmp_ref, near_ref, edge_u, mid_u, mid_v)


def theirs_kernel(
    src_ref, mask_ref, material_ref, table_ref, own_edge_u, own_mid_u, own_mid_v,
    near_ref, edge_u, acc_v_ref, acc_u_ref, keep_ref, scale_ref, root_ref, tmp_ref, mid_u, mid_v,
):
    maps(mask_ref, material_ref, table_ref, keep_ref, scale_ref, root_ref)
    acc_v_ref[...] = jnp.zeros_like(acc_v_ref)
    acc_u_ref[...] = jnp.zeros_like(acc_u_ref)
    columns(None, src_ref, lax.axis_index("col"), keep_ref, scale_ref, root_ref, tmp_ref, near_ref, edge_u, mid_u, mid_v)
    dots_uv((own_mid_u, mid_u), (own_mid_v, mid_v), acc_v_ref)
    dots_uu((own_mid_u, mid_u), acc_u_ref)
    dots_uu((own_edge_u, edge_u), acc_u_ref)


def common(block, mask):
    ncol, _, nz, ny, nx = block.shape
    near = jax.ShapeDtypeStruct((3, ny, ncol, nx), F32)
    operand = jax.ShapeDtypeStruct((3 * ny * nx // LANES, 2 * ncol, LANES), BF16)
    scratch = [
        pltpu.VMEM((ncol, 3, 3, ny, nx), F32),
        pltpu.VMEM((3, 3, ny, nx), F32),
        pltpu.VMEM((2, 3, ny, nx), F32),
        pltpu.VMEM((2, ny, nx), F32),
        pltpu.VMEM((4, 3, GROUP * ny, nx), F32),
    ]
    return near, operand, scratch, pltpu.SemaphoreType.DMA((ncol // GROUP,))


def mine(block, mask, material, table):
    near, operand, scratch, sems = common(block, mask)
    return pl.pallas_call(
        mine_kernel,
        out_shape=(near, operand, operand, operand, jax.ShapeDtypeStruct(mask.shape, F32)),
        in_specs=[HBM, VMEM, VMEM, SMEM],
        out_specs=[VMEM] * 5,
        scratch_shapes=scratch + [sems],
        compiler_params=pltpu.CompilerParams(vmem_limit_bytes=OWN_LIMIT * MIB),
        cost_estimate=pl.CostEstimate(flops=10**8, bytes_accessed=8 * 10**6, transcendentals=0),
    )(block, mask, material, table)


def theirs(other, mask, material, table, own_edge_u, own_mid_u, own_mid_v):
    ncol = other.shape[0]
    near, operand, scratch, _ = common(other, mask)
    return pl.pallas_call(
        theirs_kernel,
        out_shape=(
            near, operand,
            jax.ShapeDtypeStruct((6 * ncol, 4 * ncol), F32),
            jax.ShapeDtypeStruct((2 * ncol, 4 * ncol), F32),
        ),
        in_specs=[VMEM, VMEM, VMEM, SMEM, VMEM, VMEM, VMEM],
        out_specs=[VMEM] * 4,
        scratch_shapes=scratch[1:] + [pltpu.VMEM(operand.shape, BF16), pltpu.VMEM(operand.shape, BF16)],
        compiler_params=pltpu.CompilerParams(vmem_limit_bytes=OTHER_LIMIT * MIB),
        cost_estimate=pl.CostEstimate(flops=2 * 10**9, bytes_accessed=8 * 10**6, transcendentals=0),
    )(other, mask, material, table, own_edge_u, own_mid_u, own_mid_v)


def pack(ga, gb, gf, side, half):
    rows = slice(side * half, (side + 1) * half)
    near = slice(side * half, (side + 1) * half)
    far = slice((1 - side) * half, (2 - side) * half)
    down = lax.broadcasted_iota(jnp.int32, (half, half), 0)
    across = lax.broadcasted_iota(jnp.int32, (half, half), 1)
    aa, ba, fa = (gram[rows, near] for gram in (ga, gb, gf))
    diag = jnp.sum(jnp.where(down == across, ba, 0.0), axis=1, keepdims=True)
    mixed = jnp.where(across <= down, aa, ba)
    wide = jnp.broadcast_to(diag, (half, 256 - 5 * half))
    return jnp.concatenate([mixed, fa, ga[rows, far], gb[rows, far], gf[rows, far], wide], axis=1)


def halo_rows(near_ref, halo_ref, mask_ref, material_ref, table_ref, scale_ref, out_ref):
    core = lax.axis_index("col")
    ny, nx = mask_ref.shape[2:]
    half = near_ref.shape[2]
    root = jnp.sqrt(lookup(material_ref[3 * core], table_ref))
    for comp in range(3):
        scale_ref[comp] = mask_ref[comp, 3 * core].astype(F32) / root
    scale_ref[2] = scale_ref[2] * core.astype(F32)
    for group in range(half // GROUP):
        row = group * GROUP
        rows = pl.ds(row, GROUP)
        h1_last = None
        for y in range(ny):
            h0 = halo_ref[0, y, rows, :]
            h1 = halo_ref[1, y, rows, :]
            change = (h0, h1, minus(h1_last, h1) + behind_x(h0))
            for comp in range(3):
                value = near_ref[comp, y, rows, :] - change[comp] * scale_ref[comp, y : y + 1, :]
                put(out_ref, row, comp, y, ny, value)
            h1_last = h1


def own_kernel(near_ref, halo_ref, mask_ref, material_ref, table_ref, out_ref, scale_ref):
    halo_rows(near_ref, halo_ref, mask_ref, material_ref, table_ref, scale_ref, out_ref)


def own_rows(near, halo, mask, material, table):
    _, ny, half, nx = near.shape
    return pl.pallas_call(
        own_kernel,
        out_shape=jax.ShapeDtypeStruct((3 * ny * nx // LANES, 2 * half, LANES), BF16),
        in_specs=[VMEM, VMEM, VMEM, VMEM, SMEM],
        out_specs=VMEM,
        scratch_shapes=[pltpu.VMEM((3, ny, nx), F32)],
        compiler_params=pltpu.CompilerParams(vmem_limit_bytes=16 * MIB),
        cost_estimate=pl.CostEstimate(flops=10**7, bytes_accessed=10**6, transcendentals=0),
    )(near, halo, mask, material, table)


def finish_kernel(
    near_ref, halo_ref, mask_ref, material_ref, table_ref, own_v, own_u, other_u, acc_v_ref, acc_u_ref,
    keep_rows_ref, send_rows_ref, scale_ref, other_v, sum_v,
):
    half = near_ref.shape[2]
    n = 2 * half
    halo_rows(near_ref, halo_ref, mask_ref, material_ref, table_ref, scale_ref, other_v)
    sum_v[...] = acc_v_ref[...]
    dots_uv((own_u, other_u), (own_v, other_v), sum_v)
    cross = sum_v[0:n, 0:n]
    gf = sum_v[0:n, n : 2 * n] + (cross + cross.T)
    cross = acc_u_ref[:, n : 2 * n]
    gb = acc_u_ref[:, 0:n] + (cross + cross.T)
    rows = sum_v[n : 2 * n, :] + sum_v[2 * n : 3 * n, :]
    ga = rows[:, 0:n] + rows[:, n : 2 * n]
    keep_rows_ref[...] = pack(ga, gb, gf, 0, half)
    send_rows_ref[...] = pack(ga, gb, gf, 1, half)


def finish(near, halo, mask, material, table, own_v, own_u, other_u, acc_v, acc_u):
    _, ny, half, nx = near.shape
    rows = jax.ShapeDtypeStruct((half, 256), F32)
    return pl.pallas_call(
        finish_kernel,
        out_shape=(rows, rows),
        in_specs=[VMEM, VMEM, VMEM, VMEM, SMEM] + [VMEM] * 5,
        out_specs=[VMEM, VMEM],
        scratch_shapes=[
            pltpu.VMEM((3, ny, nx), F32),
            pltpu.VMEM(own_v.shape, BF16),
            pltpu.VMEM(acc_v.shape, F32),
        ],
        compiler_params=pltpu.CompilerParams(vmem_limit_bytes=24 * MIB),
    )(near, halo, mask, material, table, own_v, own_u, other_u, acc_v, acc_u)


def image_kernel(first, block_ref, one_ref, two_ref, mask_ref, image_ref, keep_ref):
    upper = lax.axis_index("col") == 1
    ncol, _, nz, ny, nx = block_ref.shape
    keep_ref[...] = mask_ref[...].astype(F32)
    ones = one_ref.reshape(2 * ny * ncol, nx)
    twos = two_ref.reshape(2 * ny * ncol, nx)

    def body(j, carry):
        col = first + j

        def e(comp, layer):
            return block_ref[col, comp, layer] * keep_ref[comp, layer]

        at0 = pl.ds(col, ny, stride=ncol)
        at1 = pl.ds(ny * ncol + col, ny, stride=ncol)
        one0, one1, two0, two1 = ones[at0, :], ones[at1, :], twos[at0, :], twos[at1, :]
        x, y, z = (e(comp, 0) for comp in range(3))
        lowy = x - jnp.where(upper, two0, one0)
        lowx = jnp.where(upper, two1, one1) - y
        for layer in range(nz):
            if layer + 1 < nz:
                xn, yn, zn = (e(comp, layer + 1) for comp in range(3))
            else:
                xn, yn, zn = jnp.where(upper, one0, two0), jnp.where(upper, one1, two1), None
            topx = ahead(z, 0) - (yn - y)
            topy = (xn - x) - ahead(z, 1)
            hz = ahead(y, 1) - ahead(x, 0)
            image_ref[j, 0, layer] = ((lowy - topy) - behind(hz, 0)) * keep_ref[0, layer]
            image_ref[j, 1, layer] = (behind(hz, 1) - (lowx - topx)) * keep_ref[1, layer]
            image_ref[j, 2, layer] = (behind(topx, 0) - behind(topy, 1)) * keep_ref[2, layer]
            x, y, z, lowx, lowy = xn, yn, zn, topx, topy
        return carry

    lax.fori_loop(0, image_ref.shape[0], body, 0, unroll=4)


def image_of(block, one, two, mask, first, count):
    _, _, nz, ny, nx = block.shape
    return pl.pallas_call(
        functools.partial(image_kernel, first),
        out_shape=jax.ShapeDtypeStruct((count,) + block.shape[1:], F32),
        in_specs=[VMEM] * 4,
        out_specs=VMEM,
        scratch_shapes=[pltpu.VMEM((3, nz, ny, nx), F32)],
        compiler_params=pltpu.CompilerParams(vmem_limit_bytes=16 * MIB),
        cost_estimate=pl.CostEstimate(flops=10**7, bytes_accessed=3 * 10**6, transcendentals=0),
    )(block, one, two, mask)


PARTS = 3
PIECES = 12


def residual_kernel(
    scale, rows_ref, block_ref, image0_ref, image1_ref, image2_ref, mass_ref,
    out_ref, ga_ref, gb_ref, gf_ref, theta_ref, buffer, sems,
):
    swap = lax.axis_index("col") == 1
    half, total = ga_ref.shape
    down = lax.broadcasted_iota(jnp.int32, (half, half), 0)
    across = lax.broadcasted_iota(jnp.int32, (half, half), 1)
    rows = rows_ref[...] * scale
    mixed, fa, ab, bb, fb = (rows[:, k * half : (k + 1) * half] for k in range(5))
    diag_b = rows[:, 5 * half : 5 * half + 1]
    diag_a = jnp.sum(jnp.where(down == across, mixed, 0.0), axis=1, keepdims=True)
    theta_ref[...] = jnp.broadcast_to(diag_a / diag_b, theta_ref.shape)
    ncol = block_ref.shape[0]
    per = ncol // PIECES
    images = (image0_ref, image1_ref, image2_ref)
    copies = []
    for piece in range(PIECES):
        part, start = divmod(piece * per, ncol // PARTS)
        for j in range(per):
            col = piece * per + j
            theta = theta_ref[col : col + 1, :]
            buffer[col] = images[part][start + j] - theta[None, None] * (mass_ref[...] * block_ref[col])
        some = pl.ds(piece * per, per)
        copies.append(pltpu.make_async_copy(buffer.at[some], out_ref.at[some], sems.at[piece]))
        copies[-1].start()
    flat = mixed.T
    aa = jnp.where(across <= down, mixed, flat)
    ba = jnp.where(across == down, diag_b, jnp.where(across > down, mixed, flat))
    for ref, a, b in ((ga_ref, aa, ab), (gb_ref, ba, bb), (gf_ref, fa, fb)):
        ref[...] = jnp.concatenate([jnp.where(swap, b, a), jnp.where(swap, a, b)], axis=1)
    for copy in copies:
        copy.wait()


def residual_of(rows, block, images, mass, scale):
    ncol, _, nz, ny, nx = block.shape
    gram = jax.ShapeDtypeStruct((ncol, 2 * ncol), F32)
    return pl.pallas_call(
        functools.partial(residual_kernel, scale),
        out_shape=(jax.ShapeDtypeStruct(block.shape, F32), gram, gram, gram),
        in_specs=[VMEM] * (PARTS + 3),
        out_specs=[HBM] + [VMEM] * 3,
        scratch_shapes=[
            pltpu.VMEM((ncol, nx), F32),
            pltpu.VMEM(block.shape, F32),
            pltpu.SemaphoreType.DMA((PIECES,)),
        ],
        compiler_params=pltpu.CompilerParams(vmem_limit_bytes=24 * MIB),
        cost_estimate=pl.CostEstimate(flops=2 * 10**7, bytes_accessed=15 * 10**6, transcendentals=0),
    )(rows, block, *images, mass)


def exchange_rounds(slabs):
    nz, ny, nx = GRIDS[slabs]

    def partners(size, stride, flip):
        return [i + ((i // stride % size) ^ flip) * stride - i // stride % size * stride for i in range(slabs)]

    def flips(size):
        return (3, 2, 1) if size >= 4 else (1,)

    x, y, z = ([partners(size, stride, flip) for flip in flips(size)] for size, stride in ((nx, 1), (ny, nx), (nz, nx * ny)))
    stages = [(x, y), (y, x), (z, z)]
    if nz == 8:
        halves = [partners(nz, nx * ny, 7)]
        stages.append((halves, halves))
    return [
        [
            [(2 * i, 2 * a[i]) for i in range(slabs)] + [(2 * i + 1, 2 * b[i] + 1) for i in range(slabs)]
            for a, b in zip(first, second)
        ]
        for first, second in stages
    ]


def shards(block, material, table, mask):
    slabs = lax.axis_size("space")
    ncol, _, nz, ny, nx = block.shape
    scale = 1.0 / (3.0 * nz * slabs * ny * nx)
    swap = [(0, 1), (1, 0)]
    both = ("space", "col")
    other = lax.ppermute(block, "col", swap)
    one, two = edges(block, mask)
    straight = [pair for i in range(slabs) for pair in ((2 * i, 2 * ((i + 1) % slabs)), (2 * ((i + 1) % slabs) + 1, 2 * i + 1))]
    crossed = [pair for i in range(slabs) for pair in ((2 * i + 1, 2 * ((i + 1) % slabs)), (2 * ((i + 1) % slabs), 2 * i + 1))]
    halo_own = lax.ppermute(one, both, straight)
    halo_other = lax.ppermute(two, both, crossed)
    near_own, own_u, *mid, mass = mine(block, mask, material, table)
    near_other, other_u, acc_v, acc_u = theirs(other, mask, material, table, own_u, *mid)
    near_own, near_other, halo_own = lax.optimization_barrier((near_own, near_other, halo_own))
    own_v = own_rows(near_own, halo_own, mask, material, table)
    keep_rows, send_rows = finish(near_other, halo_other, mask, material, table, own_v, own_u, other_u, acc_v, acc_u)
    rows = keep_rows + lax.ppermute(send_rows, "col", swap)
    rows, halo_other = lax.optimization_barrier((rows, halo_other))
    halo_far = lax.ppermute(halo_other, "col", swap)
    images = []
    for index, stage in enumerate(exchange_rounds(slabs)):
        arrived = [lax.ppermute(rows, both, pairs) for pairs in stage]
        if index >= 1:
            rows, halo_far = lax.optimization_barrier((rows, halo_far))
            count = ncol // PARTS
            image = image_of(block, halo_own, halo_far, mask, (index - 1) * count, count)
            arrived, image = lax.optimization_barrier((arrived, image))
            images.append(image)
        rows = rows + arrived[-1]
        if len(arrived) == 3:
            rows = rows + (arrived[1] + arrived[0])
    return residual_of(rows, block, images, mass, scale)


def solution(mesh):
    in_specs = (
        P("col", None, "space", None, None),
        P("space", None, None),
        P(),
        P(None, "space", None, None),
    )
    out_specs = (
        P("col", None, "space", None, None),
        P("col", None),
        P("col", None),
        P("col", None),
    )
    return jax.shard_map(shards, mesh=mesh, in_specs=in_specs, out_specs=out_specs, check_vma=False)
```
